256 devices in a mesh: expert: 64 (over x, y_hi, z), dp: 4 (over y_lo, core).
Axes of the slice: x: 4, y: 4 (y_hi: 2, y_lo: 2; y = y_hi * 2 + y_lo), z: 8, core: 2. Of those that a mesh axis runs over, the one named last changes fastest.
Arguments:
- tokens: bfloat16 [131072, 1280], P(('expert', 'dp')), may hold values from -24 to 24
- d_out: bfloat16 [131072, 1280], P(('expert', 'dp')), may hold values from -6 to 6
- slot_outputs: bfloat16 [1024, 8, 1280], P(('expert', 'dp')), may hold values from -6 to 6
- router: bfloat16 [1280, 8], replicated, may hold values from -6 to 6
- w_in: bfloat16 [1280, 40960], P(None, 'expert'), may hold values from -0.15625 to 0.15625
- w_out: bfloat16 [40960, 1280], P('expert'), may hold values from -0.078125 to 0.078125
Outputs:
- d_tokens: bfloat16 [131072, 1280], P(('expert', 'dp'))
- d_router: float32 [1280, 8], P(('expert', 'dp'))
- d_w_in: float32 [1280, 40960], P('dp', 'expert')
- d_w_out: float32 [40960, 1280], P('expert', 'dp')
The draws below stay inside these ranges and needn't reach their ends.
All inputs are finite; a program needn't handle non-finite values.
Results may differ from the reference program's by a relative error of at most 0.028.
Values may be sent and summed in bfloat16 or wider, within the bound.
A program may use at most 64 MiB of HBM per device.

```python
import math
import jax
import jax.numpy as jnp
from jax import lax

D = 1280
FF = 5120
EXPERTS = 8
GROUP_LEN = 128
TOKENS = 131072
GROUPS = 1024


def draw_router(key, part):
    key = jax.random.fold_in(key, 7)
    base_key, scale_key = jax.random.split(key)
    base = jnp.clip(jax.random.normal(base_key, (D, EXPERTS), jnp.float32), -4.0, 4.0)
    column_scale = jnp.exp(jax.random.uniform(scale_key, (1, EXPERTS), jnp.float32, 0.0, math.log(4.0)))
    values = jnp.clip(base * column_scale / math.sqrt(D), -6.0, 6.0)
    return values.astype(jnp.bfloat16)


def spiked(array, key, source, target, shards_of, factor):
    owner, partner = [(jnp.arange(array.shape[position]) // (array.shape[position] // shards_of)).reshape([-1 if axis == position else 1 for axis in range(array.ndim)]) for position in (source, target)]
    chosen = jax.random.permutation(key, shards_of)[partner]
    strong = (owner == chosen) | (owner == (partner + shards_of // 2) % shards_of)
    return jnp.where(strong, factor * array, array)


def block_levels(own_key, shape, pieces, least, largest):
    loudness = 1.0
    for dim, parts in pieces:
        draws = jax.random.uniform(jax.random.fold_in(jax.random.fold_in(own_key, 6), dim), (parts,), jnp.float32, least / len(pieces), largest / len(pieces))
        loudness = loudness * jnp.repeat(jnp.exp(draws), shape[dim] // parts).reshape((-1,) + (1,) * (len(shape) - 1 - dim))
    return loudness


def normal_values(key, shape, scale, bound, cuts=(), dtype=jnp.bfloat16):
    array = scale * jax.random.normal(key, shape, jnp.float32)
    if cuts:
        array = array * block_levels(key, shape, cuts, -0.22, 0.18)
    return jnp.clip(array, -bound, bound).astype(dtype)


def heavy_noise(rng, dims, scale, most, cuts, heavy, kind=jnp.bfloat16):
    drawn = scale * jax.random.normal(rng, dims, jnp.float32)
    if cuts:
        drawn = drawn * block_levels(rng, dims, cuts, -0.22, 0.18)
    return jnp.clip(spiked(drawn, jax.random.fold_in(rng, 3), *heavy), -most, most).astype(kind)


def setup_inputs(seed: int = 0) -> dict:
    key_list = jax.random.split(jax.random.key(seed), 7)
    return {
        "tokens": heavy_noise(key_list[0], (TOKENS, D), 1.0, 24.0, ((0, 256),), (0, 1, 256, 6.0)),
        "d_out": normal_values(key_list[1], (TOKENS, D), 1.0, 6.0, ((0, 256),)),
        "slot_outputs": normal_values(key_list[2], (GROUPS, EXPERTS, D), 1.0, 6.0, ((0, 256),)),
        "router": draw_router(jax.random.fold_in(key_list[6], 71), 0),
        "w_in": normal_values(key_list[4], (D, EXPERTS * FF), D ** -0.5, 0.15625, ((1, 64),)),
        "w_out": normal_values(key_list[5], (EXPERTS * FF, D), FF ** -0.5, 0.078125, ((0, 64),)),
    }


def gelu_exact(values):
    return jax.nn.gelu(values, approximate=False)

def token_front(tok_block, grad_block, router):
    logits = jnp.einsum('gld,de->gle', tok_block.astype(jnp.float32), router.astype(jnp.float32))
    dispatch = jax.nn.softmax(logits, axis=1)
    combine = jax.nn.softmax(logits, axis=2)
    dispatch_b = dispatch.astype(jnp.bfloat16)
    combine_b = combine.astype(jnp.bfloat16)
    slot_in = jnp.einsum('gle,gld->ged', dispatch_b.astype(jnp.float32), tok_block.astype(jnp.float32)).astype(jnp.bfloat16)
    slot_grad = jnp.einsum('gle,gld->ged', combine_b.astype(jnp.float32), grad_block.astype(jnp.float32)).astype(jnp.bfloat16)
    return (slot_in, slot_grad)

def token_back(tok_block, grad_block, saved_block, back_block, router):
    logits = jnp.einsum('gld,de->gle', tok_block.astype(jnp.float32), router.astype(jnp.float32))
    dispatch = jax.nn.softmax(logits, axis=1)
    combine = jax.nn.softmax(logits, axis=2)
    dispatch_b = dispatch.astype(jnp.bfloat16)
    combine_grad = jnp.einsum('gld,ged->gle', grad_block.astype(jnp.float32), saved_block.astype(jnp.float32))
    dispatch_grad = jnp.einsum('gld,ged->gle', tok_block.astype(jnp.float32), back_block.astype(jnp.float32))
    score = combine * (combine_grad - lax.optimization_barrier(jnp.sum(combine * combine_grad, axis=2, keepdims=True)))
    score = score + dispatch * (dispatch_grad - lax.optimization_barrier(jnp.sum(dispatch * dispatch_grad, axis=1, keepdims=True)))
    score_b = score.astype(jnp.bfloat16)
    direct = jnp.einsum('gle,ged->gld', dispatch_b.astype(jnp.float32), back_block.astype(jnp.float32))
    through = jnp.einsum('gle,de->gld', score_b.astype(jnp.float32), router.astype(jnp.float32))
    d_block = (direct + through).astype(jnp.bfloat16)
    router_part = jnp.einsum('gld,gle->de', tok_block.astype(jnp.float32), score_b.astype(jnp.float32))
    return (d_block, router_part)

def expert_back(operands):
    slot_in, slot_grad, first_w, second_w = operands
    pre = jnp.dot(slot_in, first_w, preferred_element_type=jnp.float32)
    hidden, pull_back = jax.vjp(gelu_exact, pre)
    hidden_b = hidden.astype(jnp.bfloat16)
    hidden_grad = jnp.dot(slot_grad, second_w.T, preferred_element_type=jnp.float32)
    pre_grad = pull_back(hidden_grad)[0].astype(jnp.bfloat16)
    grad_first = jnp.dot(slot_in.T, pre_grad, preferred_element_type=jnp.float32)
    grad_second = jnp.dot(hidden_b.T, slot_grad, preferred_element_type=jnp.float32)
    back = jnp.dot(pre_grad, first_w.T, preferred_element_type=jnp.float32)
    return (grad_first, grad_second, back)

def reference(tokens, d_out, slot_outputs, router, w_in, w_out):
    width = tokens.shape[1]
    experts = router.shape[1]
    groups = tokens.shape[0] // GROUP_LEN
    blocks = groups // 8
    tok_blocks = tokens.reshape(blocks, 8, GROUP_LEN, width)
    grad_blocks = d_out.reshape(blocks, 8, GROUP_LEN, width)
    saved_blocks = slot_outputs.reshape(blocks, 8, experts, width)
    slot_in, slot_grad = lax.map(lambda pair: token_front(pair[0], pair[1], router), (tok_blocks, grad_blocks))
    slot_in = slot_in.reshape(groups, experts, width).transpose(1, 0, 2)
    slot_grad = slot_grad.reshape(groups, experts, width).transpose(1, 0, 2)
    first_all = w_in.reshape(width, experts, FF).transpose(1, 0, 2)
    second_all = w_out.reshape(experts, FF, width)
    grad_first, grad_second, back = lax.map(expert_back, (slot_in, slot_grad, first_all, second_all))
    d_w_in = grad_first.transpose(1, 0, 2).reshape(width, experts * FF)
    d_w_out = grad_second.reshape(experts * FF, width)
    back_b = back.astype(jnp.bfloat16).transpose(1, 0, 2).reshape(blocks, 8, experts, width)
    d_blocks, router_parts = lax.map(lambda quad: token_back(quad[0], quad[1], quad[2], quad[3], router), (tok_blocks, grad_blocks, saved_blocks, back_b))
    d_tokens = d_blocks.reshape(groups * GROUP_LEN, width)
    d_router = lax.optimization_barrier(jnp.sum(router_parts, axis=0))
    return (d_tokens, d_router, d_w_in, d_w_out)
```

```python
import functools

import jax
import jax.numpy as jnp
from jax import lax
from jax.experimental import pallas as pl
from jax.experimental.pallas import tpu as pltpu
from jax.sharding import PartitionSpec as P

MESH = pl.DeviceIdType.MESH
F32 = jnp.float32
BF16 = jnp.bfloat16

D = 1280
HALF = D // 2
E = 8
Z = 8
DP = 4
GROUPS = 4
LEN = 128
TOK = GROUPS * LEN
COLS = 640
ROWS = E * GROUPS
QUARTER = D // DP
RBLOCK = D // E
RSHARE = RBLOCK // (Z * DP)


def nn(a, b):
    return lax.dot_general(a, b, (((1,), (0,)), ((), ())), preferred_element_type=F32)


def nt(a, b):
    return lax.dot_general(a, b, (((1,), (1,)), ((), ())), preferred_element_type=F32)


def tn(a, b):
    return lax.dot_general(a, b, (((0,), (0,)), ((), ())), preferred_element_type=F32)


def iota(shape, dim):
    return lax.broadcasted_iota(jnp.int32, shape, dim)


def one_hot(rows, cols, source):
    row = iota((rows, cols), 0)
    return (iota((rows, cols), 1) == source(row)).astype(F32).astype(BF16)


def bits(value, low, count):
    return lax.bitwise_and(lax.shift_right_logical(value, jnp.full_like(value, low)), jnp.full_like(value, count - 1))


def kernel(
    tok_hbm, dout_hbm, saved_hbm, router_hbm, w1_hbm, w2_hbm,
    dtok_hbm, drouter_ref, dw1_hbm, dw2_hbm,
    tok, dout, saved, router, w1, w2,
    a_send, a_recv, x, hid, pg, own, rs_out, rs_in, ret_out, ret_in,
    dw, dwb, c_in, y_out, y_in, final, dtok,
    r1_out, r1_in, r2_out, r2_in, r3_out, r3_in,
    load_sem, store_sem,
    a_ss, a_rs, g_ss, g_rs, rs_ss, rs_rs, ret_ss, ret_rs,
    c_ss, c_rs, y_ss, y_rs, r1_ss, r1_rs, r2_ss, r2_rs, r3_ss, r3_rs,
):
    expert = lax.axis_index("expert")
    dp = lax.axis_index("dp")
    a = expert // Z
    z = expert % Z
    y_lo = dp // 2
    core = dp % 2

    def at_a(j):
        return lax.rem(a + j, E)

    def at_z(j):
        return lax.rem(z + j, Z)

    def dev_a(j):
        return (at_a(j) * Z + z, dp)

    def dev_z(j):
        return (a * Z + at_z(j), dp)

    def dev_dp(j):
        return (expert, lax.rem(dp + j, DP))

    other_core = (expert, y_lo * 2 + (1 - core))
    other_y = (expert, (1 - y_lo) * 2 + core)

    def send(src, dst, ss, rs, device):
        copy = pltpu.make_async_remote_copy(
            src_ref=src, dst_ref=dst, send_sem=ss, recv_sem=rs, device_id=device, device_id_type=MESH
        )
        copy.start()
        return copy

    loads = []
    for i, (src, dst) in enumerate(
        ((tok_hbm, tok), (router_hbm, router), (dout_hbm, dout), (saved_hbm, saved), (w1_hbm, w1), (w2_hbm, w2))
    ):
        load = pltpu.make_async_copy(src, dst, load_sem.at[i])
        load.start()
        loads.append(load)
    barrier = pltpu.get_barrier_semaphore()
    for j in range(1, E):
        pl.semaphore_signal(barrier, inc=1, device_id=dev_a(j), device_id_type=MESH)
    for j in range(1, Z):
        pl.semaphore_signal(barrier, inc=1, device_id=dev_z(j), device_id_type=MESH)
    for j in range(1, DP):
        pl.semaphore_signal(barrier, inc=1, device_id=dev_dp(j), device_id_type=MESH)

    loads[0].wait()
    loads[1].wait()
    eye = one_hot(E, E, lambda r: r)
    router_t = nt(eye, router[...]).astype(BF16)
    logits = nt(router_t, tok[...])
    parts = []
    for g in range(GROUPS):
        part = logits[:, g * LEN : (g + 1) * LEN]
        part = jnp.exp(part - jnp.max(part, axis=1, keepdims=True))
        parts.append(part / jnp.sum(part, axis=1, keepdims=True))
    dispatch = jnp.concatenate(parts, axis=1)
    combine = jnp.exp(logits - jnp.max(logits, axis=0, keepdims=True))
    combine = combine / jnp.sum(combine, axis=0, keepdims=True)
    dispatch_b = dispatch.astype(BF16)
    combine_b = combine.astype(BF16)

    spread = one_hot(E * 8, E, lambda r: bits(r, 3, E))
    slot = bits(iota((E * 8, TOK), 0), 0, 8)
    group = bits(iota((E * 8, TOK), 1), 7, GROUPS)
    pick_in = jnp.where(slot == group, nn(spread, dispatch_b), 0.0).astype(BF16)
    pick_grad = jnp.where(slot == group + GROUPS, nn(spread, combine_b), 0.0).astype(BF16)
    slots = nn(pick_in, tok[...])
    loads[2].wait()
    slots = (slots + nn(pick_grad, dout[...])).reshape(E, 8, D)
    a_send[...] = jnp.concatenate([slots[:, :, :HALF], slots[:, :, HALF:]], axis=1).astype(BF16)

    pl.semaphore_wait(barrier, E + Z + DP - 3)
    a_copies = []
    for j in range(1, E):
        a_copies.append(
            send(a_send.at[at_a(j)], a_recv.at[a], a_ss.at[j - 1], a_rs.at[j - 1], dev_a(j))
        )
    a_recv[a] = a_send[a]

    loads[3].wait()
    combine_grad = jnp.concatenate(
        [nt(saved[g], dout[g * LEN : (g + 1) * LEN, :]) for g in range(GROUPS)], axis=1
    )
    score_combine = combine * (combine_grad - jnp.sum(combine * combine_grad, axis=0, keepdims=True))

    order = one_hot(
        4 * ROWS, 4 * ROWS, lambda r: bits(r, 2, 8) * 16 + bits(r, 5, 2) * 8 + bits(r, 6, 2) * 4 + bits(r, 0, 4)
    )
    for copy in a_copies:
        copy.wait_recv()
    chunk = nn(order, a_recv[...].reshape(4 * ROWS, HALF)).astype(BF16)
    for k in range(2):
        x[k, z, :, :HALF] = chunk[2 * k * ROWS : (2 * k + 1) * ROWS]
        x[k, z, :, HALF:] = chunk[(2 * k + 1) * ROWS : (2 * k + 2) * ROWS]

    hops = {}

    def hop(way, r, k):
        step = 1 if way == 0 else Z - 1
        held = at_z((Z - step) * (r - 1) % Z)
        hops[way, r, k] = send(
            x.at[k, held], x.at[k, held], g_ss.at[way, k, r - 1], g_rs.at[way, k, r - 1], dev_z(step)
        )

    rs_copies = {}

    def expert_rows(offsets):
        chunks = [at_z(d) for d in offsets]
        x_in = jnp.concatenate([x[0, c] for c in chunks], axis=0)
        x_grad = jnp.concatenate([x[1, c] for c in chunks], axis=0)
        pre = nn(x_in, w1[...])
        hidden_grad = nt(x_grad, w2[...])
        cdf = 0.5 * (1.0 + lax.erf(pre * 0.7071067811865476))
        slope = cdf + pre * jnp.exp(-0.5 * pre * pre) * 0.3989422804014327
        hidden = (pre * cdf).astype(BF16)
        pre_grad = (hidden_grad * slope).astype(BF16)
        back = nt(pre_grad, w1[...])
        for i, (d, c) in enumerate(zip(offsets, chunks)):
            rows = slice(i * ROWS, (i + 1) * ROWS)
            hid[c] = hidden[rows]
            pg[c] = pre_grad[rows]
            if d == 0:
                own[...] = back[rows]
            else:
                rs_out[c] = back[rows].astype(BF16)
                rs_copies[d] = send(
                    rs_out.at[c], rs_in.at[z], rs_ss.at[d - 1], rs_rs.at[d - 1], dev_z(d)
                )

    for k in range(2):
        for way in range(2):
            hop(way, 1, k)
    loads[4].wait()
    loads[5].wait()
    for r in range(1, 4):
        for k in range(2):
            for way in range(2):
                hops[way, r, k].wait_recv()
                if r < 3 or way == k:
                    hop(way, r + 1, k)
        expert_rows(([0] if r == 1 else []) + [Z - r, r])
    hops[0, 4, 0].wait_recv()
    hops[1, 4, 1].wait_recv()
    expert_rows([4])

    grads = (pg[...].reshape(Z * ROWS, COLS), hid[...].reshape(Z * ROWS, COLS))
    for k in range(2):
        for b in range(D // 256):
            block = tn(x[k, :, :, b * 256 : (b + 1) * 256].reshape(Z * ROWS, 256), grads[k])
            dw[k, b * 256 : (b + 1) * 256, :] = block
            dwb[k, b * 256 : (b + 1) * 256, :] = block.astype(BF16)

    def quarter(yl, c):
        return pl.ds(pl.multiple_of((yl * 2 + c) * QUARTER, QUARTER), QUARTER)

    c_copies = {}
    for i, yl in enumerate((1 - y_lo, y_lo)):
        for k in range(2):
            c_copies[i, k] = send(
                dwb.at[k, quarter(yl, 1 - core), :], c_in.at[i, k], c_ss.at[i, k], c_rs.at[i, k], other_core
            )
    y_copies = []
    for k in range(2):
        c_copies[0, k].wait_recv()
        y_out[k] = (dw[k, quarter(1 - y_lo, core), :] + c_in[0, k].astype(F32)).astype(BF16)
        y_copies.append(send(y_out.at[k], y_in.at[k], y_ss.at[k], y_rs.at[k], other_y))

    total = own[...]
    for d in (1, 7, 2, 6, 3, 5, 4):
        rs_copies[d].wait_recv()
        total = total + rs_in[at_z(Z - d)].astype(F32)
    total = total.astype(BF16)
    order = one_hot(2 * ROWS, 2 * ROWS, lambda r: bits(r, 2, 2) * ROWS + bits(r, 3, 8) * 4 + bits(r, 0, 4))
    stacked = jnp.concatenate([total[:, :HALF], total[:, HALF:]], axis=0)
    ret_out[...] = nn(order, stacked).reshape(E, 8, HALF)
    ret_copies = []
    for j in range(1, E):
        ret_copies.append(
            send(ret_out.at[at_a(j)], ret_in.at[a], ret_ss.at[j - 1], ret_rs.at[j - 1], dev_a(j))
        )
    ret_in[a] = ret_out[a]
    order = one_hot(2 * ROWS, 2 * ROWS, lambda r: bits(r, 0, 8) * 8 + bits(r, 5, 2) * 4 + bits(r, 3, 4))
    for copy in ret_copies:
        copy.wait_recv()
    mixed = nn(order, ret_in[...].reshape(2 * ROWS, HALF).astype(BF16))
    slot_grads = jnp.concatenate([mixed[:ROWS], mixed[ROWS:]], axis=1)

    parts = []
    for g in range(GROUPS):
        here = slice(g * LEN, (g + 1) * LEN)
        grad = nt(slot_grads[g * E : (g + 1) * E].astype(BF16), tok[here, :])
        weight = dispatch[:, here]
        parts.append(weight * (grad - jnp.sum(weight * grad, axis=1, keepdims=True)))
    score = (score_combine + jnp.concatenate(parts, axis=1)).astype(BF16)

    router_grad = nn(score, tok[...])
    for b in range(E):
        r1_out[b, :, :RBLOCK] = router_grad[:, b * RBLOCK : (b + 1) * RBLOCK]
        r1_out[b, :, RBLOCK:] = jnp.zeros((E, 256 - RBLOCK), F32)
    r1_copies = []
    for j in range(1, E):
        r1_copies.append(
            send(r1_out.at[at_a(j)], r1_in.at[a], r1_ss.at[j - 1], r1_rs.at[j - 1], dev_a(j))
        )

    stores = []
    router_f = router_t.astype(F32)
    for g in range(GROUPS):
        here = slice(g * LEN, (g + 1) * LEN)
        left = jnp.concatenate([dispatch_b[:, here].astype(F32), score[:, here].astype(F32)], axis=0).astype(BF16)
        right = jnp.concatenate([slot_grads[g * E : (g + 1) * E], router_f], axis=0).astype(BF16)
        dtok[here, :] = tn(left, right).astype(BF16)
        store = pltpu.make_async_copy(dtok.at[here, :], dtok_hbm.at[here, :], store_sem.at[g])
        store.start()
        stores.append(store)

    total = r1_out[a]
    for j, copy in enumerate(r1_copies, 1):
        copy.wait_recv()
        total = total + r1_in[at_a(E - j)]
    r2_out[...] = total
    r2_copies = []
    for j in range(1, Z):
        r2_copies.append(send(r2_out, r2_in.at[z], r2_ss.at[j - 1], r2_rs.at[j - 1], dev_z(j)))

    def finish(k, out):
        c_copies[1, k].wait_recv()
        y_copies[k].wait_recv()
        final[k] = dw[k, quarter(y_lo, core), :] + c_in[1, k].astype(F32) + y_in[k].astype(F32)
        store = pltpu.make_async_copy(final.at[k], out, store_sem.at[GROUPS + k])
        store.start()
        stores.append(store)

    for j, copy in enumerate(r2_copies, 1):
        copy.wait_recv()
        total = total + r2_in[at_z(Z - j)]
    r3_out[...] = total
    r3_copies = []
    for j in range(1, DP):
        r3_copies.append(send(r3_out, r3_in.at[dp], r3_ss.at[j - 1], r3_rs.at[j - 1], dev_dp(j)))
    finish(0, dw1_hbm)
    finish(1, dw2_hbm)
    for j, copy in enumerate(r3_copies, 1):
        copy.wait_recv()
        total = total + r3_in[lax.rem(dp + DP - j, DP)]
    first = (z * DP + dp) * RSHARE
    pick = (iota((E, 256), 1) == first + iota((E, 256), 0)).astype(F32)
    mine = lax.dot_general(
        pick, total, (((1,), (1,)), ((), ())), precision=lax.Precision.HIGHEST, preferred_element_type=F32
    )
    drouter_ref[...] = mine[:RSHARE]

    for store in stores:
        store.wait()
    for copy in (
        a_copies + list(hops.values()) + list(rs_copies.values()) + ret_copies
        + list(c_copies.values()) + y_copies + r1_copies + r2_copies + r3_copies
    ):
        copy.wait_send()


def shards(tokens, d_out, slot_outputs, router, w_in, w_out):
    dma = pltpu.SemaphoreType.DMA
    vmem = pltpu.VMEM
    any_space = pl.BlockSpec(memory_space=pl.ANY)
    d_tokens, d_router, d_w_in, d_w_out_t = pl.pallas_call(
        kernel,
        out_shape=(
            jax.ShapeDtypeStruct((TOK, D), BF16),
            jax.ShapeDtypeStruct((RSHARE, E), F32),
            jax.ShapeDtypeStruct((QUARTER, COLS), F32),
            jax.ShapeDtypeStruct((QUARTER, COLS), F32),
        ),
        in_specs=[any_space] * 6,
        out_specs=(any_space, pl.BlockSpec(memory_space=pltpu.VMEM), any_space, any_space),
        scratch_shapes=[
            vmem((TOK, D), BF16),
            vmem((TOK, D), BF16),
            vmem((GROUPS, E, D), BF16),
            vmem((D, E), BF16),
            vmem((D, COLS), BF16),
            vmem((COLS, D), BF16),
            vmem((E, 16, HALF), BF16),
            vmem((E, 16, HALF), BF16),
            vmem((2, Z, ROWS, D), BF16),
            vmem((Z, ROWS, COLS), BF16),
            vmem((Z, ROWS, COLS), BF16),
            vmem((ROWS, D), F32),
            vmem((Z, ROWS, D), BF16),
            vmem((Z, ROWS, D), BF16),
            vmem((E, 8, HALF), F32),
            vmem((E, 8, HALF), F32),
            vmem((2, D, COLS), F32),
            vmem((2, D, COLS), BF16),
            vmem((2, 2, QUARTER, COLS), BF16),
            vmem((2, QUARTER, COLS), BF16),
            vmem((2, QUARTER, COLS), BF16),
            vmem((2, QUARTER, COLS), F32),
            vmem((TOK, D), BF16),
            vmem((E, E, 256), F32),
            vmem((E, E, 256), F32),
            vmem((E, 256), F32),
            vmem((Z, E, 256), F32),
            vmem((E, 256), F32),
            vmem((DP, E, 256), F32),
            dma((6,)),
            dma((GROUPS + 2,)),
            dma((E - 1,)),
            dma((E - 1,)),
            dma((2, 2, 4)),
            dma((2, 2, 4)),
            dma((Z - 1,)),
            dma((Z - 1,)),
            dma((E - 1,)),
            dma((E - 1,)),
            dma((2, 2)),
            dma((2, 2)),
            dma((2,)),
            dma((2,)),
            dma((E - 1,)),
            dma((E - 1,)),
            dma((Z - 1,)),
            dma((Z - 1,)),
            dma((DP - 1,)),
            dma((DP - 1,)),
        ],
        compiler_params=pltpu.CompilerParams(
            collective_id=0, has_side_effects=True, vmem_limit_bytes=48 * 1024 * 1024
        ),
    )(tokens, d_out, slot_outputs, router, w_in, w_out)
    return (d_tokens, d_router, d_w_in, d_w_out_t.T)


def solution(mesh):
    return jax.shard_map(
        shards,
        mesh=mesh,
        in_specs=(
            P(("expert", "dp"), None),
            P(("expert", "dp"), None),
            P(("expert", "dp"), None, None),
            P(),
            P(None, "expert"),
            P("expert", None),
        ),
        out_specs=(
            P(("expert", "dp"), None),
            P(("expert", "dp"), None),
            P("dp", "expert"),
            P("expert", "dp"),
        ),
        check_vma=False,
    )
```

```python
import functools

import jax
import jax.numpy as jnp
from jax import lax
from jax.experimental import pallas as pl
from jax.experimental.pallas import tpu as pltpu
from jax.sharding import PartitionSpec as P

MESH = pl.DeviceIdType.MESH
F32 = jnp.float32
BF16 = jnp.bfloat16

D = 1280
HALF = D // 2
E = 8
Z = 8
DP = 4
GROUPS = 4
LEN = 128
TOK = GROUPS * LEN
BLOCK = 384
COLS = 640
ROWS = E * GROUPS
QUARTER = D // DP
RBLOCK = D // E
RSHARE = RBLOCK // (Z * DP)


def nn(a, b):
    return lax.dot_general(a, b, (((1,), (0,)), ((), ())), preferred_element_type=F32)


def nt(a, b):
    return lax.dot_general(a, b, (((1,), (1,)), ((), ())), preferred_element_type=F32)


def tn(a, b):
    return lax.dot_general(a, b, (((0,), (0,)), ((), ())), preferred_element_type=F32)


def iota(shape, dim):
    return lax.broadcasted_iota(jnp.int32, shape, dim)


def one_hot(rows, cols, source):
    row = iota((rows, cols), 0)
    return (iota((rows, cols), 1) == source(row)).astype(F32).astype(BF16)


def bits(value, low, count):
    return lax.bitwise_and(lax.shift_right_logical(value, jnp.full_like(value, low)), jnp.full_like(value, count - 1))


def kernel(
    tok_hbm, dout_hbm, saved_hbm, router_hbm, w1_hbm, w2_hbm,
    dtok, drouter_ref, dw1_ref, dw2_ref,
    tok, dout, saved, router, w1, w2,
    a_out, a_in, x, hid, pg, back, rs_out, rs_in, ret_out, ret_in,
    dw, dwb, c_in, y_out, y_in,
    r1_out, r1_in, r2_out, r2_in,
    load_sem,
    a_ss, a_rs, g_ss, g_rs, rs_ss, rs_rs, ret_ss, ret_rs,
    c_ss, c_rs, y_ss, y_rs, r1_ss, r1_rs, r2_ss, r2_rs,
):
    expert = lax.axis_index("expert")
    dp = lax.axis_index("dp")
    a = expert // Z
    z = expert % Z
    y_lo = dp // 2
    core = dp % 2

    def at_a(j):
        return lax.rem(a + j, E)

    def at_z(j):
        return lax.rem(z + j, Z)

    def dev_a(j):
        return (at_a(j) * Z + z, dp)

    def dev_z(j):
        return (a * Z + at_z(j), dp)

    shifts = [(i, j) for i in range(E) for j in range(DP) if i or j]
    plane = [(at_a(i) * Z + z, lax.rem(dp + j, DP)) for i, j in shifts]
    other_core = (expert, y_lo * 2 + (1 - core))
    other_y = (expert, (1 - y_lo) * 2 + core)

    def send(src, dst, ss, rs, device):
        copy = pltpu.make_async_remote_copy(
            src_ref=src, dst_ref=dst, send_sem=ss, recv_sem=rs, device_id=device, device_id_type=MESH
        )
        copy.start()
        return copy

    loads = [
        pltpu.make_async_copy(src, dst, load_sem.at[i])
        for i, (src, dst) in enumerate(
            ((tok_hbm, tok), (router_hbm, router), (dout_hbm, dout), (saved_hbm, saved), (w1_hbm, w1), (w2_hbm, w2))
        )
    ]
    loads[0].start()
    loads[1].start()
    barrier = pltpu.get_barrier_semaphore()
    for device in plane + [dev_z(j) for j in range(1, Z)]:
        pl.semaphore_signal(barrier, inc=1, device_id=device, device_id_type=MESH)

    loads[0].wait()
    loads[1].wait()
    for load in loads[2:]:
        load.start()
    logits = nt(router[...], tok[...])
    parts = []
    for g in range(GROUPS):
        part = logits[:, g * LEN : (g + 1) * LEN]
        part = jnp.exp(part - jnp.max(part, axis=1, keepdims=True))
        parts.append(part / jnp.sum(part, axis=1, keepdims=True))
    dispatch = jnp.concatenate(parts, axis=1)
    dispatch_b = dispatch.astype(BF16)
    spread = one_hot(ROWS, E, lambda r: bits(r, 2, E))
    own_group = bits(iota((ROWS, TOK), 0), 0, GROUPS) == bits(iota((ROWS, TOK), 1), 7, GROUPS)
    spread_blocks = [
        jnp.where(bits(iota((E * 16, ROWS), 0), 2, 4) == c, one_hot(E * 16, ROWS, lambda r: bits(r, 4, E) * 4 + bits(r, 0, 4)), 0.0).astype(BF16)
        for c in range(4)
    ]

    def messages(slots):
        slots = jnp.concatenate([slots, jnp.zeros((ROWS, 4 * BLOCK - D), BF16)], axis=1)
        total = nn(spread_blocks[0], slots[:, :BLOCK])
        for c in range(1, 4):
            total = total + nn(spread_blocks[c], slots[:, c * BLOCK : (c + 1) * BLOCK])
        return total.astype(BF16).reshape(E, 16, BLOCK)

    def slot_rows(weights, rows):
        pick = jnp.where(own_group, nn(spread, weights), 0.0).astype(BF16)
        return messages(nn(pick, rows).astype(BF16))

    a_copies = ([], [])

    def dispatch_rows(k):
        for j in range(1, E):
            a_copies[k].append(
                send(a_out.at[k, at_a(j)], a_in.at[k, a], a_ss.at[k, j - 1], a_rs.at[k, j - 1], dev_a(j))
            )
        a_in[k, a] = a_out[k, a]

    a_out[0] = slot_rows(dispatch_b, tok[...])
    pl.semaphore_wait(barrier, E * DP - 1 + Z - 1)
    dispatch_rows(0)
    combine = jnp.exp(logits - jnp.max(logits, axis=0, keepdims=True))
    combine = combine / jnp.sum(combine, axis=0, keepdims=True)
    loads[2].wait()
    a_out[1] = slot_rows(combine.astype(BF16), dout[...])
    dispatch_rows(1)

    order = one_hot(4 * ROWS, 4 * ROWS, lambda r: bits(r, 2, 8) * 16 + bits(r, 5, 4) * 4 + bits(r, 0, 4))
    hops = {}

    def hop(way, r, k, h):
        step = 1 if way == 0 else Z - 1
        held = at_z((Z - step) * (r - 1) % Z)
        hops[way, r, k, h] = send(
            x.at[k, h, held], x.at[k, h, held], g_ss.at[way, r - 1, k, h], g_rs.at[way, r - 1, k, h], dev_z(step)
        )

    for k in range(2):
        for copy in a_copies[k]:
            copy.wait_recv()
        chunk = nn(order, a_in[k].reshape(4 * ROWS, BLOCK)).astype(BF16)
        chunk = jnp.concatenate([chunk[c * ROWS : (c + 1) * ROWS] for c in range(4)], axis=1)
        for h in range(2):
            x[k, h, z] = chunk[:, h * HALF : (h + 1) * HALF]
            for way in range(2):
                hop(way, 1, k, h)

    loads[3].wait()
    combine_grad = jnp.concatenate(
        [nt(saved[g], dout[g * LEN : (g + 1) * LEN, :]) for g in range(GROUPS)], axis=1
    )
    score_combine = combine * (combine_grad - jnp.sum(combine * combine_grad, axis=0, keepdims=True))

    def expert_rows(offsets):
        chunks = [at_z(d) for d in offsets]
        x_in, x_grad = (
            jnp.concatenate([jnp.concatenate([x[k, h, c] for c in chunks], axis=0) for h in range(2)], axis=1)
            for k in range(2)
        )
        pre = nn(x_in, w1[...])
        hidden_grad = nt(x_grad, w2[...])
        cdf = 0.5 * (1.0 + lax.erf(pre * 0.7071067811865476))
        slope = cdf + pre * jnp.exp(-0.5 * pre * pre) * 0.3989422804014327
        hidden = (pre * cdf).astype(BF16)
        pre_grad = (hidden_grad * slope).astype(BF16)
        grads = nt(pre_grad, w1[...])
        for i, c in enumerate(chunks):
            rows = slice(i * ROWS, (i + 1) * ROWS)
            hid[c] = hidden[rows]
            pg[c] = pre_grad[rows]
            back[c] = grads[rows]

    loads[4].wait()
    loads[5].wait()
    for r in range(1, 4):
        for k in range(2):
            for h in range(2):
                for way in range(2):
                    hops[way, r, k, h].wait_recv()
                    if r < 3 or way == k:
                        hop(way, r + 1, k, h)
        expert_rows(([0] if r == 1 else []) + [Z - r, r])
    for k in range(2):
        for h in range(2):
            hops[k, 4, k, h].wait_recv()
    expert_rows([4])

    rs_copies = {}

    def half(h):
        return slice(h * HALF, (h + 1) * HALF)

    def partial(way, d, h):
        step = 1 if way == 0 else Z - 1
        value = back[at_z(step * d % Z), :, half(h)]
        if (way, d + 1, h) in rs_copies:
            rs_copies[way, d + 1, h].wait_recv()
            value = value + rs_in[way, d, h].astype(F32)
        rs_out[way, d - 1, h] = value.astype(BF16)
        rs_copies[way, d, h] = send(
            rs_out.at[way, d - 1, h], rs_in.at[way, d - 1, h], rs_ss.at[way, d - 1, h], rs_rs.at[way, d - 1, h],
            dev_z(step),
        )

    def partials(d, far):
        for way in range(2):
            partial(way, d, way if far else 1 - way)

    partials(4, True)
    partials(3, False)

    grads = (pg[...].reshape(Z * ROWS, COLS), hid[...].reshape(Z * ROWS, COLS))

    def weight_grad(k):
        for h in range(2):
            block = tn(x[k, h].reshape(Z * ROWS, HALF), grads[k])
            dw[k, h * HALF : (h + 1) * HALF, :] = block
            dwb[k, h * HALF : (h + 1) * HALF, :] = block.astype(BF16)

    def quarter(yl, c):
        return pl.ds(pl.multiple_of((yl * 2 + c) * QUARTER, QUARTER), QUARTER)

    c_copies = {}

    def to_core(i, k):
        yl = (1 - y_lo, y_lo)[i]
        c_copies[i, k] = send(
            dwb.at[k, quarter(yl, 1 - core), :], c_in.at[i, k], c_ss.at[i, k], c_rs.at[i, k], other_core
        )

    y_copies = []

    def to_chip(k):
        c_copies[0, k].wait_recv()
        y_out[k] = (dw[k, quarter(1 - y_lo, core), :] + c_in[0, k].astype(F32)).astype(BF16)
        y_copies.append(send(y_out.at[k], y_in.at[k], y_ss.at[k], y_rs.at[k], other_y))

    weight_grad(0)
    to_core(0, 0)
    partials(3, True)
    weight_grad(1)
    to_core(0, 1)
    partials(2, False)
    to_chip(0)
    to_core(1, 0)
    partials(2, True)
    to_core(1, 1)
    partials(1, False)
    partials(1, True)

    halves = []
    for h in range(2):
        value = back[z, :, half(h)]
        for way in range(2):
            rs_copies[way, 1, h].wait_recv()
            value = value + rs_in[way, 0, h].astype(F32)
        halves.append(value.astype(BF16))
    ret_out[...] = messages(jnp.concatenate(halves, axis=1))
    ret_copies = []
    for j in range(1, E):
        ret_copies.append(
            send(ret_out.at[at_a(j)], ret_in.at[a], ret_ss.at[j - 1], ret_rs.at[j - 1], dev_a(j))
        )
    ret_in[a] = ret_out[a]
    order = one_hot(4 * ROWS, 4 * ROWS, lambda r: bits(r, 0, 8) * 16 + bits(r, 5, 4) * 4 + bits(r, 3, 4))
    for copy in ret_copies:
        copy.wait_recv()
    to_chip(1)
    mixed = nn(order, ret_in[...].reshape(4 * ROWS, BLOCK))
    slot_grads = jnp.concatenate([mixed[c * ROWS : (c + 1) * ROWS] for c in range(4)], axis=1)[:, :D]

    parts = []
    for g in range(GROUPS):
        here = slice(g * LEN, (g + 1) * LEN)
        grad = nt(slot_grads[g * E : (g + 1) * E].astype(BF16), tok[here, :])
        weight = dispatch[:, here]
        parts.append(weight * (grad - jnp.sum(weight * grad, axis=1, keepdims=True)))
    score = (score_combine + jnp.concatenate(parts, axis=1)).astype(BF16)

    router_grad = nn(score, tok[...])
    for b in range(E):
        columns = router_grad[:, b * RBLOCK : (b + 1) * RBLOCK]
        columns = jnp.concatenate([columns, jnp.zeros((E, 256 - RBLOCK), F32)], axis=1)
        r1_out[b] = jnp.concatenate([columns[:, :128], columns[:, 128:]], axis=0).astype(BF16)
    r1_copies = []
    for i, device in enumerate(plane):
        r1_copies.append(
            send(r1_out.at[at_a(shifts[i][0])], r1_in.at[a * DP + dp], r1_ss.at[i], r1_rs.at[i], device)
        )

    router_f = router[...].astype(F32)
    for g in range(GROUPS):
        here = slice(g * LEN, (g + 1) * LEN)
        left = jnp.concatenate([dispatch_b[:, here].astype(F32), score[:, here].astype(F32)], axis=0).astype(BF16)
        right = jnp.concatenate([slot_grads[g * E : (g + 1) * E], router_f], axis=0).astype(BF16)
        dtok[here, :] = tn(left, right).astype(BF16)

    total = r1_out[a].astype(F32)
    for (i, j), copy in zip(shifts, r1_copies):
        copy.wait_recv()
        total = total + r1_in[at_a(E - i) * DP + lax.rem(dp + DP - j, DP)].astype(F32)
    r2_out[...] = total.astype(BF16)
    r2_copies = []
    for j in range(1, Z):
        r2_copies.append(send(r2_out, r2_in.at[z], r2_ss.at[j - 1], r2_rs.at[j - 1], dev_z(j)))

    def finish(k, out):
        c_copies[1, k].wait_recv()
        y_copies[k].wait_recv()
        out[...] = dw[k, quarter(y_lo, core), :] + c_in[1, k].astype(F32) + y_in[k].astype(F32)

    finish(0, dw1_ref)
    finish(1, dw2_ref)
    for j, copy in enumerate(r2_copies, 1):
        copy.wait_recv()
        total = total + r2_in[at_z(Z - j)].astype(F32)
    total = jnp.concatenate([total[:E], total[E:]], axis=1)
    first = (z * DP + dp) * RSHARE
    pick = (iota((E, 256), 1) == first + iota((E, 256), 0)).astype(F32)
    mine = lax.dot_general(
        pick, total, (((1,), (1,)), ((), ())), precision=lax.Precision.HIGHEST, preferred_element_type=F32
    )
    drouter_ref[...] = mine[:RSHARE]

    for copy in (
        a_copies[0] + a_copies[1] + list(hops.values()) + list(rs_copies.values()) + ret_copies
        + list(c_copies.values()) + y_copies + r1_copies + r2_copies
    ):
        copy.wait_send()


def deliver(*refs):
    sources, targets, sems = refs[:4], refs[4:8], refs[8]
    copies = [pltpu.make_async_copy(s, t, sems.at[i]) for i, (s, t) in enumerate(zip(sources, targets))]
    for copy in copies:
        copy.start()
    for copy in copies:
        copy.wait()


def shards(tokens, d_out, slot_outputs, router, w_in, w_out):
    dma = pltpu.SemaphoreType.DMA
    vmem = pltpu.VMEM
    outs = (
        jax.ShapeDtypeStruct((TOK, D), BF16),
        jax.ShapeDtypeStruct((RSHARE, E), F32),
        jax.ShapeDtypeStruct((QUARTER, COLS), F32),
        jax.ShapeDtypeStruct((QUARTER, COLS), F32),
    )
    results = pl.pallas_call(
        kernel,
        out_shape=tuple(vmem(o.shape, o.dtype) for o in outs),
        in_specs=[pl.BlockSpec(memory_space=pltpu.HBM)] * 6,
        out_specs=(pl.BlockSpec(memory_space=pltpu.VMEM),) * 4,
        scratch_shapes=[
            vmem((TOK, D), BF16),
            vmem((TOK, D), BF16),
            vmem((GROUPS, E, D), BF16),
            vmem((E, D), BF16),
            vmem((D, COLS), BF16),
            vmem((COLS, D), BF16),
            vmem((2, E, 16, BLOCK), BF16),
            vmem((2, E, 16, BLOCK), BF16),
            vmem((2, 2, Z, ROWS, HALF), BF16),
            vmem((Z, ROWS, COLS), BF16),
            vmem((Z, ROWS, COLS), BF16),
            vmem((Z, ROWS, D), F32),
            vmem((2, 4, 2, ROWS, HALF), BF16),
            vmem((2, 4, 2, ROWS, HALF), BF16),
            vmem((E, 16, BLOCK), BF16),
            vmem((E, 16, BLOCK), BF16),
            vmem((2, D, COLS), F32),
            vmem((2, D, COLS), BF16),
            vmem((2, 2, QUARTER, COLS), BF16),
            vmem((2, QUARTER, COLS), BF16),
            vmem((2, QUARTER, COLS), BF16),
            vmem((E, 16, 128), BF16),
            vmem((E * DP, 16, 128), BF16),
            vmem((16, 128), BF16),
            vmem((Z, 16, 128), BF16),
            dma((6,)),
            dma((2, E - 1)),
            dma((2, E - 1)),
            dma((2, 4, 2, 2)),
            dma((2, 4, 2, 2)),
            dma((2, 4, 2)),
            dma((2, 4, 2)),
            dma((E - 1,)),
            dma((E - 1,)),
            dma((2, 2)),
            dma((2, 2)),
            dma((2,)),
            dma((2,)),
            dma((E * DP - 1,)),
            dma((E * DP - 1,)),
            dma((Z - 1,)),
            dma((Z - 1,)),
        ],
        compiler_params=pltpu.CompilerParams(
            collective_id=0, has_side_effects=True, vmem_limit_bytes=63_900_000
        ),
    )(tokens, d_out, slot_outputs, router.T, w_in, w_out)
    d_tokens, d_router, d_w_in, d_w_out_t = pl.pallas_call(
        deliver,
        out_shape=outs,
        in_specs=[pl.BlockSpec(memory_space=pl.ANY)] * 4,
        out_specs=(pl.BlockSpec(memory_space=pl.ANY),) * 4,
        scratch_shapes=[dma((4,))],
        compiler_params=pltpu.CompilerParams(vmem_limit_bytes=1024 * 1024),
    )(*results)
    return (d_tokens, d_router, d_w_in, d_w_out_t.T)


def solution(mesh):
    return jax.shard_map(
        shards,
        mesh=mesh,
        in_specs=(
            P(("expert", "dp"), None),
            P(("expert", "dp"), None),
            P(("expert", "dp"), None, None),
            P(),
            P(None, "expert"),
            P("expert", None),
        ),
        out_specs=(
            P(("expert", "dp"), None),
            P(("expert", "dp"), None),
            P("dp", "expert"),
            P("expert", "dp"),
        ),
        check_vma=False,
    )
```

```python
import functools

import jax
import jax.numpy as jnp
from jax import lax
from jax.experimental import pallas as pl
from jax.experimental.pallas import tpu as pltpu
from jax.sharding import PartitionSpec as P

MESH = pl.DeviceIdType.MESH
F32 = jnp.float32
BF16 = jnp.bfloat16

D = 1280
HALF = D // 2
E = 8
Z = 8
DP = 4
GROUPS = 4
LEN = 128
TOK = GROUPS * LEN
BLOCK = 384
COLS = 640
ROWS = E * GROUPS
PAIR = 2 * ROWS
QUARTER = D // DP
RBLOCK = D // E
RSHARE = RBLOCK // (Z * DP)


def nn(a, b):
    return lax.dot_general(a, b, (((1,), (0,)), ((), ())), preferred_element_type=F32)


def nt(a, b):
    return lax.dot_general(a, b, (((1,), (1,)), ((), ())), preferred_element_type=F32)


def tn(a, b):
    return lax.dot_general(a, b, (((0,), (0,)), ((), ())), preferred_element_type=F32)


def iota(shape, dim):
    return lax.broadcasted_iota(jnp.int32, shape, dim)


def one_hot(rows, cols, source):
    row = iota((rows, cols), 0)
    return (iota((rows, cols), 1) == source(row)).astype(F32).astype(BF16)


def bits(value, low, count):
    return lax.bitwise_and(lax.shift_right_logical(value, jnp.full_like(value, low)), jnp.full_like(value, count - 1))


def kernel(
    tok_hbm, dout_hbm, saved_hbm, router_hbm, w1_hbm, w2_hbm,
    dtok, drouter_ref, dw1_ref, dw2_ref,
    tok, dout, saved, router, w1, w2,
    a_out, a_in, x, hid, pg, back, rs_out, rs_in, ret_out, ret_in,
    dw, c_out, c_in, y_out, y_in, y_x, y_hid, score_combine,
    r1_out, r1_in, r2_out, r2_in,
    load_sem,
    a_ss, a_rs, g_ss, g_rs, rs_ss, rs_rs, ret_ss, ret_rs,
    c_ss, c_rs, y_ss, y_rs, n_ss, n_rs, r1_ss, r1_rs, r2_ss, r2_rs,
):
    expert = lax.axis_index("expert")
    dp = lax.axis_index("dp")
    a = expert // Z
    z = expert % Z
    y_lo = dp // 2
    core = dp % 2

    def at_a(j):
        return lax.rem(a + j, E)

    def at_z(j):
        return lax.rem(z + j, Z)

    def dev_a(j):
        return (at_a(j) * Z + z, dp)

    def dev_z(j):
        return (a * Z + at_z(j), dp)

    shifts = [(i, j) for i in range(E) for j in range(DP) if i or j]
    plane = [(at_a(i) * Z + z, lax.rem(dp + j, DP)) for i, j in shifts]
    other_core = (expert, y_lo * 2 + (1 - core))
    other_chip = (expert, (1 - y_lo) * 2 + core)

    def worker(j):
        return (at_a(j) * Z + z, y_lo * 2 + 1)

    def remote(src, dst, ss, rs, device):
        return pltpu.make_async_remote_copy(
            src_ref=src, dst_ref=dst, send_sem=ss, recv_sem=rs, device_id=device, device_id_type=MESH
        )

    def send(*args):
        remote(*args).start()

    def arrived(ref, sem):
        remote(ref, ref, sem, sem, other_core).wait_recv()

    def sent(ref, sem):
        remote(ref, ref, sem, sem, other_core).wait_send()

    loads = [
        pltpu.make_async_copy(src, dst, load_sem.at[i])
        for i, (src, dst) in enumerate(
            ((tok_hbm, tok), (router_hbm, router), (dout_hbm, dout), (saved_hbm, saved), (w1_hbm, w1), (w2_hbm, w2))
        )
    ]
    loads[0].start()
    loads[1].start()
    barrier = pltpu.get_barrier_semaphore()
    for device in plane + [dev_z(j) for j in range(1, Z)]:
        pl.semaphore_signal(barrier, inc=1, device_id=device, device_id_type=MESH)

    loads[0].wait()
    loads[1].wait()
    loads[2].start()
    loads[3].start()

    @pl.when(core == 1)
    def _():
        loads[4].start()
        loads[5].start()

    logits = nt(router[...], tok[...])
    parts = []
    for g in range(GROUPS):
        part = logits[:, g * LEN : (g + 1) * LEN]
        part = jnp.exp(part - jnp.max(part, axis=1, keepdims=True))
        parts.append(part / jnp.sum(part, axis=1, keepdims=True))
    dispatch = jnp.concatenate(parts, axis=1)
    dispatch_b = dispatch.astype(BF16)
    spread = one_hot(ROWS, E, lambda r: bits(r, 2, E))
    own_group = bits(iota((ROWS, TOK), 0), 0, GROUPS) == bits(iota((ROWS, TOK), 1), 7, GROUPS)
    spread_blocks = [
        jnp.where(bits(iota((E * 16, ROWS), 0), 2, 4) == c, one_hot(E * 16, ROWS, lambda r: bits(r, 4, E) * 4 + bits(r, 0, 4)), 0.0).astype(BF16)
        for c in range(4)
    ]

    def messages(slots):
        slots = jnp.concatenate([slots, jnp.zeros((ROWS, 4 * BLOCK - D), BF16)], axis=1)
        total = nn(spread_blocks[0], slots[:, :BLOCK])
        for c in range(1, 4):
            total = total + nn(spread_blocks[c], slots[:, c * BLOCK : (c + 1) * BLOCK])
        return total.astype(BF16).reshape(E, 16, BLOCK)

    def slot_rows(weights, rows):
        pick = jnp.where(own_group, nn(spread, weights), 0.0).astype(BF16)
        return messages(nn(pick, rows).astype(BF16))

    def dispatch_rows(k):
        for j in range(1, E):
            send(a_out.at[k, at_a(j)], a_in.at[k, core, a], a_ss.at[k, j], a_rs.at[k, core, j], worker(j))

        @pl.when(core == 0)
        def _():
            send(a_out.at[k, a], a_in.at[k, 0, a], a_ss.at[k, 0], a_rs.at[k, 0, 0], worker(0))

        @pl.when(core == 1)
        def _():
            a_in[k, 1, a] = a_out[k, a]

    a_out[0] = slot_rows(dispatch_b, tok[...])
    pl.semaphore_wait(barrier, E * DP - 1 + Z - 1)
    dispatch_rows(0)
    combine = jnp.exp(logits - jnp.max(logits, axis=0, keepdims=True))
    combine = combine / jnp.sum(combine, axis=0, keepdims=True)
    loads[2].wait()
    a_out[1] = slot_rows(combine.astype(BF16), dout[...])
    dispatch_rows(1)

    def early_score():
        loads[3].wait()
        combine_grad = jnp.concatenate(
            [nt(saved[g], dout[g * LEN : (g + 1) * LEN, :]) for g in range(GROUPS)], axis=1
        )
        score_combine[...] = combine * (combine_grad - jnp.sum(combine * combine_grad, axis=0, keepdims=True))

    def hop(way, r, k, h):
        step = 1 if way == 0 else Z - 1
        held = at_z((Z - step) * (r - 1) % Z)
        send(x.at[k, h, held], x.at[k, h, held], g_ss.at[way, r - 1, k, h], g_rs.at[way, r - 1, k, h], dev_z(step))

    def hop_arrived(way, r, k, h):
        arrived(x.at[k, h, 0], g_rs.at[way, r - 1, k, h])

    def expert_rows(offsets):
        chunks = [at_z(d) for d in offsets]
        for d, c in zip(offsets, chunks):
            send(x.at[1, 1 - y_lo, c], y_x.at[c], n_ss.at[0, d], n_rs.at[0, d], other_chip)
        x_in, x_grad = (
            jnp.concatenate([jnp.concatenate([x[k, h, c] for c in chunks], axis=0) for h in range(2)], axis=1)
            for k in range(2)
        )
        pre = nn(x_in, w1[...])
        hidden_grad = nt(x_grad, w2[...])
        cdf = 0.5 * (1.0 + lax.erf(pre * 0.7071067811865476))
        slope = cdf + pre * jnp.exp(-0.5 * pre * pre) * 0.3989422804014327
        hidden = (pre * cdf).astype(BF16)
        pre_grad = (hidden_grad * slope).astype(BF16)
        grads = nt(pre_grad, w1[...])
        for i, c in enumerate(chunks):
            rows = slice(i * PAIR, (i + 1) * PAIR)
            hid[c] = hidden[rows]
            pg[c] = pre_grad[rows]
            back[c] = grads[rows]
        for d, c in zip(offsets, chunks):
            send(hid.at[c], y_hid.at[c], n_ss.at[1, d], n_rs.at[1, d], other_chip)

    def half(h):
        return slice(h * HALF, (h + 1) * HALF)

    def partial(way, d, h):
        step = 1 if way == 0 else Z - 1
        value = back[at_z(step * d % Z), :, half(h)]
        if d < 3 or (d == 3 and h == way):
            arrived(rs_in.at[way, d, h], rs_rs.at[way, d, h])
            value = value + rs_in[way, d, h].astype(F32)
        rs_out[way, d - 1, h] = value.astype(BF16)
        send(
            rs_out.at[way, d - 1, h], rs_in.at[way, d - 1, h], rs_ss.at[way, d - 1, h], rs_rs.at[way, d - 1, h],
            dev_z(step),
        )

    def partials(d, far):
        for way in range(2):
            partial(way, d, way if far else 1 - way)

    def rows_dot(rows, grads):
        return tn(rows.reshape(Z * PAIR, HALF), grads.reshape(Z * PAIR, COLS))

    def share(k, grad):
        dw[k] = grad[QUARTER:]
        c_out[k] = grad[:QUARTER].astype(BF16)
        send(c_out.at[k], c_in.at[k], c_ss.at[k], c_rs.at[k], other_core)

    def other_in():
        y_out[...] = rows_dot(x[0, 1 - y_lo], pg[...]).astype(BF16).reshape(2, QUARTER, COLS)
        for c in range(2):
            send(y_out.at[c], y_in, y_ss.at[c], y_rs, (expert, (1 - y_lo) * 2 + c))

    def own_in():
        share(0, rows_dot(x[0, y_lo], pg[...]))

    def own_out():
        for d in range(Z):
            arrived(y_x.at[0], n_rs.at[0, d])
            arrived(y_hid.at[0], n_rs.at[1, d])
        share(1, rows_dot(x[1, y_lo], hid[...]) + rows_dot(y_x[...], y_hid[...]))

    @pl.when(core == 0)
    def _():
        early_score()

    @pl.when(core == 1)
    def _():
        order = one_hot(
            4 * PAIR, 4 * PAIR,
            lambda r: bits(r, 5, 2) * 128 + bits(r, 2, 8) * 16 + bits(r, 6, 4) * 4 + bits(r, 0, 4),
        )
        for k in range(2):
            for c in range(2):
                for j in range(c, E):
                    arrived(a_in.at[k, c, 0], a_rs.at[k, c, j])
            chunk = nn(order, a_in[k].reshape(4 * PAIR, BLOCK)).astype(BF16)
            chunk = jnp.concatenate([chunk[b * PAIR : (b + 1) * PAIR] for b in range(4)], axis=1)
            for h in range(2):
                x[k, h, z] = chunk[:, half(h)]
                for way in range(2):
                    hop(way, 1, k, h)
        early_score()
        loads[4].wait()
        loads[5].wait()
        for r in range(1, 4):
            for k in range(2):
                for h in range(2):
                    for way in range(2):
                        hop_arrived(way, r, k, h)
                        if r < 3 or way == k:
                            hop(way, r + 1, k, h)
            expert_rows(([0] if r == 1 else []) + [Z - r, r])
        for k in range(2):
            for h in range(2):
                hop_arrived(k, 4, k, h)
        expert_rows([4])

        partials(4, True)
        partials(3, False)
        other_in()
        partials(3, True)
        partials(2, False)
        own_in()
        partials(2, True)
        own_out()
        partials(1, False)
        partials(1, True)

        halves = []
        for h in range(2):
            value = back[z, :, half(h)]
            for way in range(2):
                arrived(rs_in.at[way, 0, h], rs_rs.at[way, 0, h])
                value = value + rs_in[way, 0, h].astype(F32)
            halves.append(value.astype(BF16))
        total = jnp.concatenate(halves, axis=1)
        for c in range(2):
            ret_out[c] = messages(total[c * ROWS : (c + 1) * ROWS])
            for j in range(c, E):
                send(
                    ret_out.at[c, at_a(j)], ret_in.at[a], ret_ss.at[c, j], ret_rs.at[j],
                    (at_a(j) * Z + z, y_lo * 2 + c),
                )
        ret_in[a] = ret_out[1, a]

    order = one_hot(4 * ROWS, 4 * ROWS, lambda r: bits(r, 0, 8) * 16 + bits(r, 5, 4) * 4 + bits(r, 3, 4))
    for j in range(1, E):
        arrived(ret_in.at[0], ret_rs.at[j])

    @pl.when(core == 0)
    def _():
        arrived(ret_in.at[0], ret_rs.at[0])

    mixed = nn(order, ret_in[...].reshape(4 * ROWS, BLOCK))
    slot_grads = jnp.concatenate([mixed[c * ROWS : (c + 1) * ROWS] for c in range(4)], axis=1)[:, :D]

    parts = []
    for g in range(GROUPS):
        here = slice(g * LEN, (g + 1) * LEN)
        grad = nt(slot_grads[g * E : (g + 1) * E].astype(BF16), tok[here, :])
        weight = dispatch[:, here]
        parts.append(weight * (grad - jnp.sum(weight * grad, axis=1, keepdims=True)))
    score = (score_combine[...] + jnp.concatenate(parts, axis=1)).astype(BF16)

    router_grad = nn(score, tok[...])
    for b in range(E):
        columns = router_grad[:, b * RBLOCK : (b + 1) * RBLOCK]
        columns = jnp.concatenate([columns, jnp.zeros((E, 256 - RBLOCK), F32)], axis=1)
        r1_out[b] = jnp.concatenate([columns[:, :128], columns[:, 128:]], axis=0).astype(BF16)
    for i, device in enumerate(plane):
        send(r1_out.at[at_a(shifts[i][0])], r1_in.at[a * DP + dp], r1_ss.at[i], r1_rs.at[i], device)

    router_f = router[...].astype(F32)
    for g in range(GROUPS):
        here = slice(g * LEN, (g + 1) * LEN)
        left = jnp.concatenate([dispatch_b[:, here].astype(F32), score[:, here].astype(F32)], axis=0).astype(BF16)
        right = jnp.concatenate([slot_grads[g * E : (g + 1) * E], router_f], axis=0).astype(BF16)
        dtok[here, :] = tn(left, right).astype(BF16)

    total = r1_out[a].astype(F32)
    for n, (i, j) in enumerate(shifts):
        arrived(r1_in.at[0], r1_rs.at[n])
        total = total + r1_in[at_a(E - i) * DP + lax.rem(dp + DP - j, DP)].astype(F32)
    r2_out[...] = total.astype(BF16)
    for j in range(1, Z):
        send(r2_out, r2_in.at[z], r2_ss.at[j - 1], r2_rs.at[j - 1], dev_z(j))

    arrived(y_in, y_rs)

    @pl.when(core == 0)
    def _():
        for k in range(2):
            arrived(c_in.at[k], c_rs.at[k])
        dw1_ref[...] = c_in[0].astype(F32) + y_in[...].astype(F32)
        dw2_ref[...] = c_in[1].astype(F32)

    @pl.when(core == 1)
    def _():
        dw1_ref[...] = dw[0] + y_in[...].astype(F32)
        dw2_ref[...] = dw[1]

    for j in range(1, Z):
        arrived(r2_in.at[0], r2_rs.at[j - 1])
        total = total + r2_in[at_z(Z - j)].astype(F32)
    total = jnp.concatenate([total[:E], total[E:]], axis=1)
    first = (z * DP + dp) * RSHARE
    pick = (iota((E, 256), 1) == first + iota((E, 256), 0)).astype(F32)
    mine = lax.dot_general(
        pick, total, (((1,), (1,)), ((), ())), precision=lax.Precision.HIGHEST, preferred_element_type=F32
    )
    drouter_ref[...] = mine[:RSHARE]

    for k in range(2):
        for j in range(1, E):
            sent(a_out.at[k, 0], a_ss.at[k, j])
    for n in range(E * DP - 1):
        sent(r1_out.at[0], r1_ss.at[n])
    for n in range(Z - 1):
        sent(r2_out, r2_ss.at[n])

    @pl.when(core == 0)
    def _():
        for k in range(2):
            sent(a_out.at[k, 0], a_ss.at[k, 0])

    @pl.when(core == 1)
    def _():
        for way in range(2):
            for k in range(2):
                for h in range(2):
                    for r in range(1, 5 if way == k else 4):
                        sent(x.at[k, h, 0], g_ss.at[way, r - 1, k, h])
            for h in range(2):
                for d in range(1, 5 if way == h else 4):
                    sent(rs_out.at[way, d - 1, h], rs_ss.at[way, d - 1, h])
        for k in range(2):
            sent(c_out.at[k], c_ss.at[k])
            sent(y_out.at[k], y_ss.at[k])
            for d in range(Z):
                sent(hid.at[0], n_ss.at[k, d])
        for c in range(2):
            for j in range(c, E):
                sent(ret_out.at[c, 0], ret_ss.at[c, j])


def deliver(*refs):
    sources, targets, sems = refs[:4], refs[4:8], refs[8]
    copies = [pltpu.make_async_copy(s, t, sems.at[i]) for i, (s, t) in enumerate(zip(sources, targets))]
    for copy in copies:
        copy.start()
    for copy in copies:
        copy.wait()


def shards(tokens, d_out, slot_outputs, router, w_in, w_out):
    dma = pltpu.SemaphoreType.DMA
    vmem = pltpu.VMEM
    outs = (
        jax.ShapeDtypeStruct((TOK, D), BF16),
        jax.ShapeDtypeStruct((RSHARE, E), F32),
        jax.ShapeDtypeStruct((QUARTER, COLS), F32),
        jax.ShapeDtypeStruct((QUARTER, COLS), F32),
    )
    results = pl.pallas_call(
        kernel,
        out_shape=tuple(vmem(o.shape, o.dtype) for o in outs),
        in_specs=[pl.BlockSpec(memory_space=pltpu.HBM)] * 6,
        out_specs=(pl.BlockSpec(memory_space=pltpu.VMEM),) * 4,
        scratch_shapes=[
            vmem((TOK, D), BF16),
            vmem((TOK, D), BF16),
            vmem((GROUPS, E, D), BF16),
            vmem((E, D), BF16),
            vmem((D, COLS), BF16),
            vmem((COLS, D), BF16),
            vmem((2, E, 16, BLOCK), BF16),
            vmem((2, 2, E, 16, BLOCK), BF16),
            vmem((2, 2, Z, PAIR, HALF), BF16),
            vmem((Z, PAIR, COLS), BF16),
            vmem((Z, PAIR, COLS), BF16),
            vmem((Z, PAIR, D), F32),
            vmem((2, 4, 2, PAIR, HALF), BF16),
            vmem((2, 4, 2, PAIR, HALF), BF16),
            vmem((2, E, 16, BLOCK), BF16),
            vmem((E, 16, BLOCK), BF16),
            vmem((2, QUARTER, COLS), F32),
            vmem((2, QUARTER, COLS), BF16),
            vmem((2, QUARTER, COLS), BF16),
            vmem((2, QUARTER, COLS), BF16),
            vmem((QUARTER, COLS), BF16),
            vmem((Z, PAIR, HALF), BF16),
            vmem((Z, PAIR, COLS), BF16),
            vmem((E, TOK), F32),
            vmem((E, 16, 128), BF16),
            vmem((E * DP, 16, 128), BF16),
            vmem((16, 128), BF16),
            vmem((Z, 16, 128), BF16),
            dma((6,)),
            dma((2, E)),
            dma((2, 2, E)),
            dma((2, 4, 2, 2)),
            dma((2, 4, 2, 2)),
            dma((2, 4, 2)),
            dma((2, 4, 2)),
            dma((2, E)),
            dma((E,)),
            dma((2,)),
            dma((2,)),
            dma((2,)),
            dma,
            dma((2, Z)),
            dma((2, Z)),
            dma((E * DP - 1,)),
            dma((E * DP - 1,)),
            dma((Z - 1,)),
            dma((Z - 1,)),
        ],
        compiler_params=pltpu.CompilerParams(
            collective_id=0, has_side_effects=True, vmem_limit_bytes=63_900_000
        ),
    )(tokens, d_out, slot_outputs, router.T, w_in, w_out)
    d_tokens, d_router, d_w_in, d_w_out_t = pl.pallas_call(
        deliver,
        out_shape=outs,
        in_specs=[pl.BlockSpec(memory_space=pl.ANY)] * 4,
        out_specs=(pl.BlockSpec(memory_space=pl.ANY),) * 4,
        scratch_shapes=[dma((4,))],
        compiler_params=pltpu.CompilerParams(vmem_limit_bytes=1024 * 1024),
    )(*results)
    return (d_tokens, d_router, d_w_in, d_w_out_t.T)


def solution(mesh):
    return jax.shard_map(
        shards,
        mesh=mesh,
        in_specs=(
            P(("expert", "dp"), None),
            P(("expert", "dp"), None),
            P(("expert", "dp"), None, None),
            P(),
            P(None, "expert"),
            P("expert", None),
        ),
        out_specs=(
            P(("expert", "dp"), None),
            P(("expert", "dp"), None),
            P("dp", "expert"),
            P("expert", "dp"),
        ),
        check_vma=False,
    )
```

```python
import functools

import jax
import jax.numpy as jnp
from jax import lax
from jax.experimental import pallas as pl
from jax.experimental.pallas import tpu as pltpu
from jax.sharding import PartitionSpec as P

MESH = pl.DeviceIdType.MESH
F32 = jnp.float32
BF16 = jnp.bfloat16

D = 1280
HALF = D // 2
E = 8
Z = 8
DP = 4
GROUPS = 4
LEN = 128
TOK = GROUPS * LEN
BLOCK = 384
COLS = 640
ROWS = E * GROUPS
PAIR = 2 * ROWS
QUARTER = D // DP
RBLOCK = D // E
RSHARE = RBLOCK // (Z * DP)


def nn(a, b):
    return lax.dot_general(a, b, (((1,), (0,)), ((), ())), preferred_element_type=F32)


def nt(a, b):
    return lax.dot_general(a, b, (((1,), (1,)), ((), ())), preferred_element_type=F32)


def tn(a, b):
    return lax.dot_general(a, b, (((0,), (0,)), ((), ())), preferred_element_type=F32)


def iota(shape, dim):
    return lax.broadcasted_iota(jnp.int32, shape, dim)


def one_hot(rows, cols, source):
    row = iota((rows, cols), 0)
    return (iota((rows, cols), 1) == source(row)).astype(F32).astype(BF16)


def bits(value, low, count):
    return lax.bitwise_and(lax.shift_right_logical(value, jnp.full_like(value, low)), jnp.full_like(value, count - 1))


def kernel(
    tok_hbm, dout_hbm, saved_hbm, router_hbm, w1_hbm, w2_hbm,
    dtok, drouter_ref, dw1_ref, dw2_ref,
    tok, dout, saved, router, w1, w2,
    a_out, a_in, x, hid, pg, back, rs_out, rs_in, ret_out, ret_in,
    dw, c_out, c_in, y_out, y_in, y_x, y_hid, score_combine,
    r1_out, r1_in, r2_out, r2_in,
    load_sem,
    a_ss, a_rs, g_ss, g_rs, rs_ss, rs_rs, ret_ss, ret_rs,
    c_ss, c_rs, y_ss, y_rs, n_ss, n_rs, r1_ss, r1_rs, r2_ss, r2_rs,
):
    expert = lax.axis_index("expert")
    dp = lax.axis_index("dp")
    a = expert // Z
    z = expert % Z
    y_lo = dp // 2
    core = dp % 2

    def at_a(j):
        return lax.rem(a + j, E)

    def at_z(j):
        return lax.rem(z + j, Z)

    def dev_a(j):
        return (at_a(j) * Z + z, dp)

    def dev_z(j):
        return (a * Z + at_z(j), dp)

    shifts = [(i, j) for i in range(E) for j in range(DP) if i or j]
    plane = [(at_a(i) * Z + z, lax.rem(dp + j, DP)) for i, j in shifts]
    other_core = (expert, y_lo * 2 + (1 - core))
    other_chip = (expert, (1 - y_lo) * 2 + core)

    def worker(j):
        return (at_a(j) * Z + z, y_lo * 2 + 1)

    def remote(src, dst, ss, rs, device):
        return pltpu.make_async_remote_copy(
            src_ref=src, dst_ref=dst, send_sem=ss, recv_sem=rs, device_id=device, device_id_type=MESH
        )

    def send(*args):
        remote(*args).start()

    def arrived(ref, sem):
        remote(ref, ref, sem, sem, other_core).wait_recv()

    def sent(ref, sem):
        remote(ref, ref, sem, sem, other_core).wait_send()

    loads = [
        pltpu.make_async_copy(src, dst, load_sem.at[i])
        for i, (src, dst) in enumerate(
            ((router_hbm, router), (dout_hbm, dout), (saved_hbm, saved), (w1_hbm, w1), (w2_hbm, w2))
        )
    ]
    groups = [pl.ds(g * LEN, LEN) for g in range(GROUPS)]
    token_loads = [
        pltpu.make_async_copy(tok_hbm.at[here, :], tok.at[here, :], load_sem.at[5 + g]) for g, here in enumerate(groups)
    ]
    loads[0].start()
    for load in token_loads:
        load.start()
    barrier = pltpu.get_barrier_semaphore()
    for device in plane + [dev_z(j) for j in range(1, Z)]:
        pl.semaphore_signal(barrier, inc=1, device_id=device, device_id_type=MESH)

    loads[0].wait()
    loads[1].start()
    loads[2].start()

    @pl.when(core == 1)
    def _():
        loads[3].start()
        loads[4].start()

    logits, parts = [], []
    for load, here in zip(token_loads, groups):
        load.wait()
        logits.append(nt(router[...], tok[here, :]))
    for part in logits:
        part = jnp.exp(part - jnp.max(part, axis=1, keepdims=True))
        parts.append(part / jnp.sum(part, axis=1, keepdims=True))
    logits = jnp.concatenate(logits, axis=1)
    dispatch = jnp.concatenate(parts, axis=1)
    dispatch_b = dispatch.astype(BF16)
    spread = one_hot(ROWS, E, lambda r: bits(r, 2, E))
    own_group = bits(iota((ROWS, TOK), 0), 0, GROUPS) == bits(iota((ROWS, TOK), 1), 7, GROUPS)
    spread_blocks = [
        jnp.where(bits(iota((E * 16, ROWS), 0), 2, 4) == c, one_hot(E * 16, ROWS, lambda r: bits(r, 4, E) * 4 + bits(r, 0, 4)), 0.0).astype(BF16)
        for c in range(4)
    ]

    def messages(slots):
        slots = jnp.concatenate([slots, jnp.zeros((ROWS, 4 * BLOCK - D), BF16)], axis=1)
        total = nn(spread_blocks[0], slots[:, :BLOCK])
        for c in range(1, 4):
            total = total + nn(spread_blocks[c], slots[:, c * BLOCK : (c + 1) * BLOCK])
        return total.astype(BF16).reshape(E, 16, BLOCK)

    def slot_rows(weights, rows):
        pick = jnp.where(own_group, nn(spread, weights), 0.0).astype(BF16)
        return messages(nn(pick, rows).astype(BF16))

    def dispatch_rows(k):
        for j in range(1, E):
            send(a_out.at[k, at_a(j)], a_in.at[k, core, a], a_ss.at[k, j], a_rs.at[k, core, j], worker(j))

        @pl.when(core == 0)
        def _():
            send(a_out.at[k, a], a_in.at[k, 0, a], a_ss.at[k, 0], a_rs.at[k, 0, 0], worker(0))

        @pl.when(core == 1)
        def _():
            a_in[k, 1, a] = a_out[k, a]

    a_out[0] = slot_rows(dispatch_b, tok[...])
    pl.semaphore_wait(barrier, E * DP - 1 + Z - 1)
    dispatch_rows(0)
    combine = jnp.exp(logits - jnp.max(logits, axis=0, keepdims=True))
    combine = combine / jnp.sum(combine, axis=0, keepdims=True)
    loads[1].wait()
    a_out[1] = slot_rows(combine.astype(BF16), dout[...])
    dispatch_rows(1)

    def early_score():
        loads[2].wait()
        combine_grad = jnp.concatenate(
            [nt(saved[g], dout[g * LEN : (g + 1) * LEN, :]) for g in range(GROUPS)], axis=1
        )
        score_combine[...] = combine * (combine_grad - jnp.sum(combine * combine_grad, axis=0, keepdims=True))

    def hop(way, r, k, h):
        step = 1 if way == 0 else Z - 1
        held = at_z((Z - step) * (r - 1) % Z)
        send(x.at[k, h, held], x.at[k, h, held], g_ss.at[way, r - 1, k, h], g_rs.at[way, r - 1, k, h], dev_z(step))

    def hop_arrived(way, r, k, h):
        arrived(x.at[k, h, 0], g_rs.at[way, r - 1, k, h])

    def expert_rows(offsets):
        chunks = [at_z(d) for d in offsets]
        for d, c in zip(offsets, chunks):
            send(x.at[1, 1 - y_lo, c], y_x.at[c], n_ss.at[0, d], n_rs.at[0, d], other_chip)
        x_in, x_grad = (
            jnp.concatenate([jnp.concatenate([x[k, h, c] for c in chunks], axis=0) for h in range(2)], axis=1)
            for k in range(2)
        )
        pre = nn(x_in, w1[...])
        hidden_grad = nt(x_grad, w2[...])
        cdf = 0.5 * (1.0 + lax.erf(pre * 0.7071067811865476))
        slope = cdf + pre * jnp.exp(-0.5 * pre * pre) * 0.3989422804014327
        hidden = (pre * cdf).astype(BF16)
        pre_grad = (hidden_grad * slope).astype(BF16)
        grads = nt(pre_grad, w1[...])
        for i, c in enumerate(chunks):
            rows = slice(i * PAIR, (i + 1) * PAIR)
            hid[c] = hidden[rows]
            pg[c] = pre_grad[rows]
            back[c] = grads[rows]
        for d, c in zip(offsets, chunks):
            send(hid.at[c], y_hid.at[c], n_ss.at[1, d], n_rs.at[1, d], other_chip)

    def half(h):
        return slice(h * HALF, (h + 1) * HALF)

    def partial(way, d, h):
        step = 1 if way == 0 else Z - 1
        value = back[at_z(step * d % Z), :, half(h)]
        if d < 3:
            arrived(rs_in.at[way, d, h], rs_rs.at[way, d, h])
            value = value + rs_in[way, d, h].astype(F32)
        if d == 1 and h == way:
            arrived(rs_in.at[way, 3, h], rs_rs.at[way, 3, h])
            value = value + rs_in[way, 3, h].astype(F32)
        rs_out[way, d - 1, h] = value.astype(BF16)
        send(
            rs_out.at[way, d - 1, h], rs_in.at[way, d - 1, h], rs_ss.at[way, d - 1, h], rs_rs.at[way, d - 1, h],
            dev_z(3 * step % Z if d == 4 else step),
        )

    def partials(d, far):
        for way in range(2):
            partial(way, d, way if far else 1 - way)

    def rows_dot(rows, grads):
        return tn(rows.reshape(Z * PAIR, HALF), grads.reshape(Z * PAIR, COLS))

    def share(k, grad):
        dw[k] = grad[QUARTER:]
        c_out[k] = grad[:QUARTER].astype(BF16)
        send(c_out.at[k], c_in.at[k], c_ss.at[k], c_rs.at[k], other_core)

    def other_in():
        y_out[...] = rows_dot(x[0, 1 - y_lo], pg[...]).astype(BF16).reshape(2, QUARTER, COLS)
        for c in range(2):
            send(y_out.at[c], y_in, y_ss.at[c], y_rs, (expert, (1 - y_lo) * 2 + c))

    def own_in():
        share(0, rows_dot(x[0, y_lo], pg[...]))

    def own_out():
        for d in range(Z):
            arrived(y_x.at[0], n_rs.at[0, d])
            arrived(y_hid.at[0], n_rs.at[1, d])
        share(1, rows_dot(x[1, y_lo], hid[...]) + rows_dot(y_x[...], y_hid[...]))

    @pl.when(core == 0)
    def _():
        early_score()

    @pl.when(core == 1)
    def _():
        order = one_hot(
            4 * PAIR, 4 * PAIR,
            lambda r: bits(r, 5, 2) * 128 + bits(r, 2, 8) * 16 + bits(r, 6, 4) * 4 + bits(r, 0, 4),
        )
        for k in range(2):
            for c in range(2):
                for j in range(c, E):
                    arrived(a_in.at[k, c, 0], a_rs.at[k, c, j])
            chunk = nn(order, a_in[k].reshape(4 * PAIR, BLOCK)).astype(BF16)
            chunk = jnp.concatenate([chunk[b * PAIR : (b + 1) * PAIR] for b in range(4)], axis=1)
            for h in range(2):
                x[k, h, z] = chunk[:, half(h)]
                for way in range(2):
                    hop(way, 1, k, h)
        early_score()
        loads[3].wait()
        loads[4].wait()
        for r in range(1, 4):
            for k in range(2):
                for h in range(2):
                    for way in range(2):
                        hop_arrived(way, r, k, h)
                        if r < 3 or way == k:
                            hop(way, r + 1, k, h)
            expert_rows(([0] if r == 1 else []) + [Z - r, r])
        partials(3, False)
        partials(3, True)
        for k in range(2):
            for h in range(2):
                hop_arrived(k, 4, k, h)
        expert_rows([4])

        partials(4, True)
        other_in()
        partials(2, False)
        partials(2, True)
        partials(1, False)
        partials(1, True)

        halves = []
        for h in range(2):
            value = back[z, :, half(h)]
            for way in range(2):
                arrived(rs_in.at[way, 0, h], rs_rs.at[way, 0, h])
                value = value + rs_in[way, 0, h].astype(F32)
            halves.append(value.astype(BF16))
        total = jnp.concatenate(halves, axis=1)
        for c in range(2):
            ret_out[c] = messages(total[c * ROWS : (c + 1) * ROWS])
            for j in range(c, E):
                send(
                    ret_out.at[c, at_a(j)], ret_in.at[a], ret_ss.at[c, j], ret_rs.at[j],
                    (at_a(j) * Z + z, y_lo * 2 + c),
                )
        ret_in[a] = ret_out[1, a]
        own_in()
        own_out()

    order = one_hot(4 * ROWS, 4 * ROWS, lambda r: bits(r, 0, 8) * 16 + bits(r, 5, 4) * 4 + bits(r, 3, 4))
    for j in range(1, E):
        arrived(ret_in.at[0], ret_rs.at[j])

    @pl.when(core == 0)
    def _():
        arrived(ret_in.at[0], ret_rs.at[0])

    mixed = nn(order, ret_in[...].reshape(4 * ROWS, BLOCK))
    slot_grads = jnp.concatenate([mixed[c * ROWS : (c + 1) * ROWS] for c in range(4)], axis=1)[:, :D]

    parts = []
    for g in range(GROUPS):
        here = slice(g * LEN, (g + 1) * LEN)
        grad = nt(slot_grads[g * E : (g + 1) * E].astype(BF16), tok[here, :])
        weight = dispatch[:, here]
        parts.append(weight * (grad - jnp.sum(weight * grad, axis=1, keepdims=True)))
    score = (score_combine[...] + jnp.concatenate(parts, axis=1)).astype(BF16)

    router_grad = nn(score, tok[...])
    for b in range(E):
        columns = router_grad[:, b * RBLOCK : (b + 1) * RBLOCK]
        columns = jnp.concatenate([columns, jnp.zeros((E, 256 - RBLOCK), F32)], axis=1)
        r1_out[b] = jnp.concatenate([columns[:, :128], columns[:, 128:]], axis=0).astype(BF16)
    for i, device in enumerate(plane):
        send(r1_out.at[at_a(shifts[i][0])], r1_in.at[a * DP + dp], r1_ss.at[i], r1_rs.at[i], device)

    router_f = router[...].astype(F32)
    for g in range(GROUPS):
        here = slice(g * LEN, (g + 1) * LEN)
        left = jnp.concatenate([dispatch_b[:, here].astype(F32), score[:, here].astype(F32)], axis=0).astype(BF16)
        right = jnp.concatenate([slot_grads[g * E : (g + 1) * E], router_f], axis=0).astype(BF16)
        dtok[here, :] = tn(left, right).astype(BF16)

    for k in range(2):
        for j in range(1, E):
            sent(a_out.at[k, 0], a_ss.at[k, j])

    @pl.when(core == 0)
    def _():
        for k in range(2):
            sent(a_out.at[k, 0], a_ss.at[k, 0])

    @pl.when(core == 1)
    def _():
        for way in range(2):
            for k in range(2):
                for h in range(2):
                    for r in range(1, 5 if way == k else 4):
                        sent(x.at[k, h, 0], g_ss.at[way, r - 1, k, h])
            for h in range(2):
                for d in range(1, 5 if way == h else 4):
                    sent(rs_out.at[way, d - 1, h], rs_ss.at[way, d - 1, h])
        for k in range(2):
            sent(c_out.at[k], c_ss.at[k])
            sent(y_out.at[k], y_ss.at[k])
            for d in range(Z):
                sent(hid.at[0], n_ss.at[k, d])
        for c in range(2):
            for j in range(c, E):
                sent(ret_out.at[c, 0], ret_ss.at[c, j])

    total = r1_out[a].astype(F32)
    for n, (i, j) in enumerate(shifts):
        arrived(r1_in.at[0], r1_rs.at[n])
        total = total + r1_in[at_a(E - i) * DP + lax.rem(dp + DP - j, DP)].astype(F32)
    r2_out[...] = total.astype(BF16)
    for j in range(1, Z):
        send(r2_out, r2_in.at[z], r2_ss.at[j - 1], r2_rs.at[j - 1], dev_z(j))

    for n in range(E * DP - 1):
        sent(r1_out.at[0], r1_ss.at[n])
    arrived(y_in, y_rs)

    @pl.when(core == 0)
    def _():
        for k in range(2):
            arrived(c_in.at[k], c_rs.at[k])
        dw1_ref[...] = c_in[0].astype(F32) + y_in[...].astype(F32)
        dw2_ref[...] = c_in[1].astype(F32)

    @pl.when(core == 1)
    def _():
        dw1_ref[...] = dw[0] + y_in[...].astype(F32)
        dw2_ref[...] = dw[1]

    for j in range(1, Z):
        arrived(r2_in.at[0], r2_rs.at[j - 1])
        total = total + r2_in[at_z(Z - j)].astype(F32)
    total = jnp.concatenate([total[:E], total[E:]], axis=1)
    first = (z * DP + dp) * RSHARE
    pick = (iota((E, 256), 1) == first + iota((E, 256), 0)).astype(F32)
    mine = lax.dot_general(
        pick, total, (((1,), (1,)), ((), ())), precision=lax.Precision.HIGHEST, preferred_element_type=F32
    )
    drouter_ref[...] = mine[:RSHARE]

    for n in range(Z - 1):
        sent(r2_out, r2_ss.at[n])


def deliver(*refs):
    sources, targets, sems = refs[:4], refs[4:8], refs[8]
    copies = [pltpu.make_async_copy(s, t, sems.at[i]) for i, (s, t) in enumerate(zip(sources, targets))]
    for copy in copies:
        copy.start()
    for copy in copies:
        copy.wait()


def shards(tokens, d_out, slot_outputs, router, w_in, w_out):
    dma = pltpu.SemaphoreType.DMA
    vmem = pltpu.VMEM
    outs = (
        jax.ShapeDtypeStruct((TOK, D), BF16),
        jax.ShapeDtypeStruct((RSHARE, E), F32),
        jax.ShapeDtypeStruct((QUARTER, COLS), F32),
        jax.ShapeDtypeStruct((QUARTER, COLS), F32),
    )
    results = pl.pallas_call(
        kernel,
        out_shape=tuple(vmem(o.shape, o.dtype) for o in outs),
        in_specs=[pl.BlockSpec(memory_space=pltpu.HBM)] * 6,
        out_specs=(pl.BlockSpec(memory_space=pltpu.VMEM),) * 4,
        scratch_shapes=[
            vmem((TOK, D), BF16),
            vmem((TOK, D), BF16),
            vmem((GROUPS, E, D), BF16),
            vmem((E, D), BF16),
            vmem((D, COLS), BF16),
            vmem((COLS, D), BF16),
            vmem((2, E, 16, BLOCK), BF16),
            vmem((2, 2, E, 16, BLOCK), BF16),
            vmem((2, 2, Z, PAIR, HALF), BF16),
            vmem((Z, PAIR, COLS), BF16),
            vmem((Z, PAIR, COLS), BF16),
            vmem((Z, PAIR, D), F32),
            vmem((2, 4, 2, PAIR, HALF), BF16),
            vmem((2, 4, 2, PAIR, HALF), BF16),
            vmem((2, E, 16, BLOCK), BF16),
            vmem((E, 16, BLOCK), BF16),
            vmem((2, QUARTER, COLS), F32),
            vmem((2, QUARTER, COLS), BF16),
            vmem((2, QUARTER, COLS), BF16),
            vmem((2, QUARTER, COLS), BF16),
            vmem((QUARTER, COLS), BF16),
            vmem((Z, PAIR, HALF), BF16),
            vmem((Z, PAIR, COLS), BF16),
            vmem((E, TOK), F32),
            vmem((E, 16, 128), BF16),
            vmem((E * DP, 16, 128), BF16),
            vmem((16, 128), BF16),
            vmem((Z, 16, 128), BF16),
            dma((5 + GROUPS,)),
            dma((2, E)),
            dma((2, 2, E)),
            dma((2, 4, 2, 2)),
            dma((2, 4, 2, 2)),
            dma((2, 4, 2)),
            dma((2, 4, 2)),
            dma((2, E)),
            dma((E,)),
            dma((2,)),
            dma((2,)),
            dma((2,)),
            dma,
            dma((2, Z)),
            dma((2, Z)),
            dma((E * DP - 1,)),
            dma((E * DP - 1,)),
            dma((Z - 1,)),
            dma((Z - 1,)),
        ],
        compiler_params=pltpu.CompilerParams(
            collective_id=0, has_side_effects=True, vmem_limit_bytes=63_900_000
        ),
    )(tokens, d_out, slot_outputs, router.T, w_in, w_out)
    d_tokens, d_router, d_w_in, d_w_out_t = pl.pallas_call(
        deliver,
        out_shape=outs,
        in_specs=[pl.BlockSpec(memory_space=pl.ANY)] * 4,
        out_specs=(pl.BlockSpec(memory_space=pl.ANY),) * 4,
        scratch_shapes=[dma((4,))],
        compiler_params=pltpu.CompilerParams(vmem_limit_bytes=1024 * 1024),
    )(*results)
    return (d_tokens, d_router, d_w_in, d_w_out_t.T)


def solution(mesh):
    return jax.shard_map(
        shards,
        mesh=mesh,
        in_specs=(
            P(("expert", "dp"), None),
            P(("expert", "dp"), None),
            P(("expert", "dp"), None, None),
            P(),
            P(None, "expert"),
            P("expert", None),
        ),
        out_specs=(
            P(("expert", "dp"), None),
            P(("expert", "dp"), None),
            P("dp", "expert"),
            P("expert", "dp"),
        ),
        check_vma=False,
    )
```

```python
import functools

import jax
import jax.numpy as jnp
from jax import lax
from jax.experimental import pallas as pl
from jax.experimental.pallas import tpu as pltpu
from jax.sharding import PartitionSpec as P

MESH = pl.DeviceIdType.MESH
F32 = jnp.float32
BF16 = jnp.bfloat16

D = 1280
HALF = D // 2
E = 8
Z = 8
DP = 4
GROUPS = 4
LEN = 128
TOK = GROUPS * LEN
BLOCK = 384
COLS = 640
ROWS = E * GROUPS
PAIR = 2 * ROWS
QUARTER = D // DP
RBLOCK = D // E
RSHARE = RBLOCK // (Z * DP)
FAR_A = (5, 3, 4, 2, 6, 1, 7, 0)
FAR_Z = (4, 3, 5, 2, 6, 1, 7)
FAR_DP = (3, 2, 1, 0)


def nn(a, b):
    return lax.dot_general(a, b, (((1,), (0,)), ((), ())), preferred_element_type=F32)


def nt(a, b):
    return lax.dot_general(a, b, (((1,), (1,)), ((), ())), preferred_element_type=F32)


def tn(a, b):
    return lax.dot_general(a, b, (((0,), (0,)), ((), ())), preferred_element_type=F32)


def iota(shape, dim):
    return lax.broadcasted_iota(jnp.int32, shape, dim)


def one_hot(rows, cols, source):
    row = iota((rows, cols), 0)
    return (iota((rows, cols), 1) == source(row)).astype(F32).astype(BF16)


def bits(value, low, count):
    return lax.bitwise_and(lax.shift_right_logical(value, jnp.full_like(value, low)), jnp.full_like(value, count - 1))


def kernel(
    tok_hbm, dout_hbm, saved_hbm, router_hbm, w1_hbm, w2_hbm,
    dtok, drouter_ref, dw1_ref, dw2_ref,
    tok, dout, saved, router, w1, w2,
    a_out, a_in, x, hid, pg, back, rs_out, rs_in, ret_out, ret_in,
    dw, c_out, c_in, y_out, y_in, y_x, y_hid, score_combine,
    r1_out, r1_in, r2_out, r2_in,
    load_sem,
    a_ss, a_rs, g_ss, g_rs, rs_ss, rs_rs, ret_ss, ret_rs,
    c_ss, c_rs, y_ss, y_rs, n_ss, n_rs, r1_ss, r1_rs, r2_ss, r2_rs,
):
    expert = lax.axis_index("expert")
    dp = lax.axis_index("dp")
    a = expert // Z
    z = expert % Z
    y_lo = dp // 2
    core = dp % 2

    def at_a(j):
        return lax.rem(a + j, E)

    def at_z(j):
        return lax.rem(z + j, Z)

    def dev_a(j):
        return (at_a(j) * Z + z, dp)

    def dev_z(j):
        return (a * Z + at_z(j), dp)

    shifts = [(i, j) for i in FAR_A for j in FAR_DP if i or j]
    plane = [(at_a(i) * Z + z, lax.rem(dp + j, DP)) for i, j in shifts]
    other_core = (expert, y_lo * 2 + (1 - core))
    other_chip = (expert, (1 - y_lo) * 2 + core)

    def worker(j):
        return (at_a(j) * Z + z, y_lo * 2 + 1)

    def remote(src, dst, ss, rs, device):
        return pltpu.make_async_remote_copy(
            src_ref=src, dst_ref=dst, send_sem=ss, recv_sem=rs, device_id=device, device_id_type=MESH
        )

    def send(*args):
        remote(*args).start()

    def arrived(ref, sem):
        remote(ref, ref, sem, sem, other_core).wait_recv()

    def sent(ref, sem):
        remote(ref, ref, sem, sem, other_core).wait_send()

    loads = [
        pltpu.make_async_copy(src, dst, load_sem.at[i])
        for i, (src, dst) in enumerate(
            ((router_hbm, router), (dout_hbm, dout), (saved_hbm, saved), (w1_hbm, w1), (w2_hbm, w2))
        )
    ]
    groups = [pl.ds(g * LEN, LEN) for g in range(GROUPS)]
    token_loads = [
        pltpu.make_async_copy(tok_hbm.at[here, :], tok.at[here, :], load_sem.at[5 + g]) for g, here in enumerate(groups)
    ]
    loads[0].start()
    for load in token_loads:
        load.start()
    barrier = pltpu.get_barrier_semaphore()
    for device in plane + [dev_z(j) for j in range(1, Z)]:
        pl.semaphore_signal(barrier, inc=1, device_id=device, device_id_type=MESH)

    loads[0].wait()
    loads[1].start()
    loads[2].start()

    @pl.when(core == 1)
    def _():
        loads[3].start()
        loads[4].start()

    logits, parts = [], []
    for load, here in zip(token_loads, groups):
        load.wait()
        logits.append(nt(router[...], tok[here, :]))
    for part in logits:
        part = jnp.exp(part - jnp.max(part, axis=1, keepdims=True))
        parts.append(part / jnp.sum(part, axis=1, keepdims=True))
    logits = jnp.concatenate(logits, axis=1)
    dispatch = jnp.concatenate(parts, axis=1)
    dispatch_b = dispatch.astype(BF16)
    spread = one_hot(ROWS, E, lambda r: bits(r, 2, E))
    own_group = bits(iota((ROWS, TOK), 0), 0, GROUPS) == bits(iota((ROWS, TOK), 1), 7, GROUPS)
    spread_blocks = [
        jnp.where(bits(iota((E * 16, ROWS), 0), 2, 4) == c, one_hot(E * 16, ROWS, lambda r: bits(r, 4, E) * 4 + bits(r, 0, 4)), 0.0).astype(BF16)
        for c in range(4)
    ]

    def messages(slots):
        slots = jnp.concatenate([slots, jnp.zeros((ROWS, 4 * BLOCK - D), BF16)], axis=1)
        total = nn(spread_blocks[0], slots[:, :BLOCK])
        for c in range(1, 4):
            total = total + nn(spread_blocks[c], slots[:, c * BLOCK : (c + 1) * BLOCK])
        return total.astype(BF16).reshape(E, 16, BLOCK)

    def slot_rows(weights, rows):
        pick = jnp.where(own_group, nn(spread, weights), 0.0).astype(BF16)
        return messages(nn(pick, rows).astype(BF16))

    def dispatch_rows(k):
        for j in FAR_A[:-1]:
            send(a_out.at[k, at_a(j)], a_in.at[k, core, a], a_ss.at[k, j], a_rs.at[k, core, j], worker(j))

        @pl.when(core == 0)
        def _():
            send(a_out.at[k, a], a_in.at[k, 0, a], a_ss.at[k, 0], a_rs.at[k, 0, 0], worker(0))

        @pl.when(core == 1)
        def _():
            a_in[k, 1, a] = a_out[k, a]

    a_out[0] = slot_rows(dispatch_b, tok[...])
    pl.semaphore_wait(barrier, E * DP - 1 + Z - 1)
    dispatch_rows(0)
    combine = jnp.exp(logits - jnp.max(logits, axis=0, keepdims=True))
    combine = combine / jnp.sum(combine, axis=0, keepdims=True)
    loads[1].wait()
    a_out[1] = slot_rows(combine.astype(BF16), dout[...])
    dispatch_rows(1)

    def early_score():
        loads[2].wait()
        combine_grad = jnp.concatenate(
            [nt(saved[g], dout[g * LEN : (g + 1) * LEN, :]) for g in range(GROUPS)], axis=1
        )
        score_combine[...] = combine * (combine_grad - jnp.sum(combine * combine_grad, axis=0, keepdims=True))

    def hop(way, r, k, h):
        step = 1 if way == 0 else Z - 1
        held = at_z((Z - step) * (r - 1) % Z)
        send(x.at[k, h, held], x.at[k, h, held], g_ss.at[way, r - 1, k, h], g_rs.at[way, r - 1, k, h], dev_z(step))

    def hop_arrived(way, r, k, h):
        arrived(x.at[k, h, 0], g_rs.at[way, r - 1, k, h])

    def expert_rows(offsets):
        chunks = [at_z(d) for d in offsets]
        for d, c in zip(offsets, chunks):
            send(x.at[1, 1 - y_lo, c], y_x.at[c], n_ss.at[0, d], n_rs.at[0, d], other_chip)
        x_in, x_grad = (
            jnp.concatenate([jnp.concatenate([x[k, h, c] for c in chunks], axis=0) for h in range(2)], axis=1)
            for k in range(2)
        )
        pre = nn(x_in, w1[...])
        hidden_grad = nt(x_grad, w2[...])
        cdf = 0.5 * (1.0 + lax.erf(pre * 0.7071067811865476))
        slope = cdf + pre * jnp.exp(-0.5 * pre * pre) * 0.3989422804014327
        hidden = (pre * cdf).astype(BF16)
        pre_grad = (hidden_grad * slope).astype(BF16)
        grads = nt(pre_grad, w1[...])
        for i, c in enumerate(chunks):
            rows = slice(i * PAIR, (i + 1) * PAIR)
            hid[c] = hidden[rows]
            pg[c] = pre_grad[rows]
            back[c] = grads[rows]
        for d, c in zip(offsets, chunks):
            send(hid.at[c], y_hid.at[c], n_ss.at[1, d], n_rs.at[1, d], other_chip)

    def half(h):
        return slice(h * HALF, (h + 1) * HALF)

    def partial(way, d, h):
        step = 1 if way == 0 else Z - 1
        value = back[at_z(step * d % Z), :, half(h)]
        if d < 3:
            arrived(rs_in.at[way, d, h], rs_rs.at[way, d, h])
            value = value + rs_in[way, d, h].astype(F32)
        if d == 1 and h == way:
            arrived(rs_in.at[way, 3, h], rs_rs.at[way, 3, h])
            value = value + rs_in[way, 3, h].astype(F32)
        rs_out[way, d - 1, h] = value.astype(BF16)
        send(
            rs_out.at[way, d - 1, h], rs_in.at[way, d - 1, h], rs_ss.at[way, d - 1, h], rs_rs.at[way, d - 1, h],
            dev_z(3 * step % Z if d == 4 else step),
        )

    def partials(d, far):
        for way in range(2):
            partial(way, d, way if far else 1 - way)

    def rows_dot(rows, grads):
        return tn(rows.reshape(Z * PAIR, HALF), grads.reshape(Z * PAIR, COLS))

    def share(k, grad):
        dw[k] = grad[QUARTER:]
        c_out[k] = grad[:QUARTER].astype(BF16)
        send(c_out.at[k], c_in.at[k], c_ss.at[k], c_rs.at[k], other_core)

    def other_in():
        y_out[...] = rows_dot(x[0, 1 - y_lo], pg[...]).astype(BF16).reshape(2, QUARTER, COLS)
        for c in range(2):
            send(y_out.at[c], y_in, y_ss.at[c], y_rs, (expert, (1 - y_lo) * 2 + c))

    def own_in():
        share(0, rows_dot(x[0, y_lo], pg[...]))

    def own_out():
        for d in range(Z):
            arrived(y_x.at[0], n_rs.at[0, d])
            arrived(y_hid.at[0], n_rs.at[1, d])
        share(1, rows_dot(x[1, y_lo], hid[...]) + rows_dot(y_x[...], y_hid[...]))

    @pl.when(core == 0)
    def _():
        early_score()

    @pl.when(core == 1)
    def _():
        order = one_hot(
            4 * PAIR, 4 * PAIR,
            lambda r: bits(r, 5, 2) * 128 + bits(r, 2, 8) * 16 + bits(r, 6, 4) * 4 + bits(r, 0, 4),
        )
        for k in range(2):
            for c in range(2):
                for j in range(c, E):
                    arrived(a_in.at[k, c, 0], a_rs.at[k, c, j])
            chunk = nn(order, a_in[k].reshape(4 * PAIR, BLOCK)).astype(BF16)
            chunk = jnp.concatenate([chunk[b * PAIR : (b + 1) * PAIR] for b in range(4)], axis=1)
            for h in range(2):
                x[k, h, z] = chunk[:, half(h)]
                for way in range(2):
                    hop(way, 1, k, h)
        early_score()
        loads[3].wait()
        loads[4].wait()
        for r in range(1, 4):
            for k in range(2):
                for h in range(2):
                    for way in range(2):
                        hop_arrived(way, r, k, h)
                        if r < 3 or way == k:
                            hop(way, r + 1, k, h)
            expert_rows(([0] if r == 1 else []) + [Z - r, r])
        partials(3, False)
        partials(3, True)
        for k in range(2):
            for h in range(2):
                hop_arrived(k, 4, k, h)
        expert_rows([4])

        partials(4, True)
        other_in()
        partials(2, False)
        partials(2, True)
        partials(1, False)
        partials(1, True)

        halves = []
        for h in range(2):
            value = back[z, :, half(h)]
            for way in range(2):
                arrived(rs_in.at[way, 0, h], rs_rs.at[way, 0, h])
                value = value + rs_in[way, 0, h].astype(F32)
            halves.append(value.astype(BF16))
        total = jnp.concatenate(halves, axis=1)
        for c in range(2):
            ret_out[c] = messages(total[c * ROWS : (c + 1) * ROWS])
            for j in FAR_A[: E - c]:
                send(
                    ret_out.at[c, at_a(j)], ret_in.at[a], ret_ss.at[c, j], ret_rs.at[j],
                    (at_a(j) * Z + z, y_lo * 2 + c),
                )
        ret_in[a] = ret_out[1, a]
        own_in()
        own_out()

    order = one_hot(4 * ROWS, 4 * ROWS, lambda r: bits(r, 0, 8) * 16 + bits(r, 5, 4) * 4 + bits(r, 3, 4))
    for j in range(1, E):
        arrived(ret_in.at[0], ret_rs.at[j])

    @pl.when(core == 0)
    def _():
        arrived(ret_in.at[0], ret_rs.at[0])

    mixed = nn(order, ret_in[...].reshape(4 * ROWS, BLOCK))
    slot_grads = jnp.concatenate([mixed[c * ROWS : (c + 1) * ROWS] for c in range(4)], axis=1)[:, :D]

    parts = []
    for g in range(GROUPS):
        here = slice(g * LEN, (g + 1) * LEN)
        grad = nt(slot_grads[g * E : (g + 1) * E].astype(BF16), tok[here, :])
        weight = dispatch[:, here]
        parts.append(weight * (grad - jnp.sum(weight * grad, axis=1, keepdims=True)))
    score = (score_combine[...] + jnp.concatenate(parts, axis=1)).astype(BF16)

    router_grad = nn(score, tok[...])
    for b in range(E):
        columns = router_grad[:, b * RBLOCK : (b + 1) * RBLOCK]
        columns = jnp.concatenate([columns, jnp.zeros((E, 256 - RBLOCK), F32)], axis=1)
        r1_out[b] = jnp.concatenate([columns[:, :128], columns[:, 128:]], axis=0).astype(BF16)
    for i, device in enumerate(plane):
        send(r1_out.at[at_a(shifts[i][0])], r1_in.at[a * DP + dp], r1_ss.at[i], r1_rs.at[i], device)

    router_f = router[...].astype(F32)
    for g in range(GROUPS):
        here = slice(g * LEN, (g + 1) * LEN)
        left = jnp.concatenate([dispatch_b[:, here].astype(F32), score[:, here].astype(F32)], axis=0).astype(BF16)
        right = jnp.concatenate([slot_grads[g * E : (g + 1) * E], router_f], axis=0).astype(BF16)
        dtok[here, :] = tn(left, right).astype(BF16)

    for k in range(2):
        for j in range(1, E):
            sent(a_out.at[k, 0], a_ss.at[k, j])

    @pl.when(core == 0)
    def _():
        for k in range(2):
            sent(a_out.at[k, 0], a_ss.at[k, 0])

    @pl.when(core == 1)
    def _():
        for way in range(2):
            for k in range(2):
                for h in range(2):
                    for r in range(1, 5 if way == k else 4):
                        sent(x.at[k, h, 0], g_ss.at[way, r - 1, k, h])
            for h in range(2):
                for d in range(1, 5 if way == h else 4):
                    sent(rs_out.at[way, d - 1, h], rs_ss.at[way, d - 1, h])
        for k in range(2):
            sent(c_out.at[k], c_ss.at[k])
            sent(y_out.at[k], y_ss.at[k])
            for d in range(Z):
                sent(hid.at[0], n_ss.at[k, d])
        for c in range(2):
            for j in range(c, E):
                sent(ret_out.at[c, 0], ret_ss.at[c, j])

    total = r1_out[a].astype(F32)
    for n, (i, j) in enumerate(shifts):
        arrived(r1_in.at[0], r1_rs.at[n])
        total = total + r1_in[at_a(E - i) * DP + lax.rem(dp + DP - j, DP)].astype(F32)
    r2_out[...] = total.astype(BF16)
    for j in FAR_Z:
        send(r2_out, r2_in.at[z], r2_ss.at[j - 1], r2_rs.at[j - 1], dev_z(j))

    for n in range(E * DP - 1):
        sent(r1_out.at[0], r1_ss.at[n])
    arrived(y_in, y_rs)

    @pl.when(core == 0)
    def _():
        for k in range(2):
            arrived(c_in.at[k], c_rs.at[k])
        dw1_ref[...] = c_in[0].astype(F32) + y_in[...].astype(F32)
        dw2_ref[...] = c_in[1].astype(F32)

    @pl.when(core == 1)
    def _():
        dw1_ref[...] = dw[0] + y_in[...].astype(F32)
        dw2_ref[...] = dw[1]

    for j in range(1, Z):
        arrived(r2_in.at[0], r2_rs.at[j - 1])
        total = total + r2_in[at_z(Z - j)].astype(F32)
    total = jnp.concatenate([total[:E], total[E:]], axis=1)
    first = (z * DP + dp) * RSHARE
    pick = (iota((E, 256), 1) == first + iota((E, 256), 0)).astype(F32)
    mine = lax.dot_general(
        pick, total, (((1,), (1,)), ((), ())), precision=lax.Precision.HIGHEST, preferred_element_type=F32
    )
    drouter_ref[...] = mine[:RSHARE]

    for n in range(Z - 1):
        sent(r2_out, r2_ss.at[n])


def deliver(*refs):
    sources, targets, sems = refs[:4], refs[4:8], refs[8]
    copies = [pltpu.make_async_copy(s, t, sems.at[i]) for i, (s, t) in enumerate(zip(sources, targets))]
    for copy in copies:
        copy.start()
    for copy in copies:
        copy.wait()


def shards(tokens, d_out, slot_outputs, router, w_in, w_out):
    dma = pltpu.SemaphoreType.DMA
    vmem = pltpu.VMEM
    outs = (
        jax.ShapeDtypeStruct((TOK, D), BF16),
        jax.ShapeDtypeStruct((RSHARE, E), F32),
        jax.ShapeDtypeStruct((QUARTER, COLS), F32),
        jax.ShapeDtypeStruct((QUARTER, COLS), F32),
    )
    results = pl.pallas_call(
        kernel,
        out_shape=tuple(vmem(o.shape, o.dtype) for o in outs),
        in_specs=[pl.BlockSpec(memory_space=pltpu.HBM)] * 6,
        out_specs=(pl.BlockSpec(memory_space=pltpu.VMEM),) * 4,
        scratch_shapes=[
            vmem((TOK, D), BF16),
            vmem((TOK, D), BF16),
            vmem((GROUPS, E, D), BF16),
            vmem((E, D), BF16),
            vmem((D, COLS), BF16),
            vmem((COLS, D), BF16),
            vmem((2, E, 16, BLOCK), BF16),
            vmem((2, 2, E, 16, BLOCK), BF16),
            vmem((2, 2, Z, PAIR, HALF), BF16),
            vmem((Z, PAIR, COLS), BF16),
            vmem((Z, PAIR, COLS), BF16),
            vmem((Z, PAIR, D), F32),
            vmem((2, 4, 2, PAIR, HALF), BF16),
            vmem((2, 4, 2, PAIR, HALF), BF16),
            vmem((2, E, 16, BLOCK), BF16),
            vmem((E, 16, BLOCK), BF16),
            vmem((2, QUARTER, COLS), F32),
            vmem((2, QUARTER, COLS), BF16),
            vmem((2, QUARTER, COLS), BF16),
            vmem((2, QUARTER, COLS), BF16),
            vmem((QUARTER, COLS), BF16),
            vmem((Z, PAIR, HALF), BF16),
            vmem((Z, PAIR, COLS), BF16),
            vmem((E, TOK), F32),
            vmem((E, 16, 128), BF16),
            vmem((E * DP, 16, 128), BF16),
            vmem((16, 128), BF16),
            vmem((Z, 16, 128), BF16),
            dma((5 + GROUPS,)),
            dma((2, E)),
            dma((2, 2, E)),
            dma((2, 4, 2, 2)),
            dma((2, 4, 2, 2)),
            dma((2, 4, 2)),
            dma((2, 4, 2)),
            dma((2, E)),
            dma((E,)),
            dma((2,)),
            dma((2,)),
            dma((2,)),
            dma,
            dma((2, Z)),
            dma((2, Z)),
            dma((E * DP - 1,)),
            dma((E * DP - 1,)),
            dma((Z - 1,)),
            dma((Z - 1,)),
        ],
        compiler_params=pltpu.CompilerParams(
            collective_id=0, has_side_effects=True, vmem_limit_bytes=63_900_000
        ),
    )(tokens, d_out, slot_outputs, router.T, w_in, w_out)
    d_tokens, d_router, d_w_in, d_w_out_t = pl.pallas_call(
        deliver,
        out_shape=outs,
        in_specs=[pl.BlockSpec(memory_space=pl.ANY)] * 4,
        out_specs=(pl.BlockSpec(memory_space=pl.ANY),) * 4,
        scratch_shapes=[dma((4,))],
        compiler_params=pltpu.CompilerParams(vmem_limit_bytes=1024 * 1024),
    )(*results)
    return (d_tokens, d_router, d_w_in, d_w_out_t.T)


def solution(mesh):
    return jax.shard_map(
        shards,
        mesh=mesh,
        in_specs=(
            P(("expert", "dp"), None),
            P(("expert", "dp"), None),
            P(("expert", "dp"), None, None),
            P(),
            P(None, "expert"),
            P("expert", None),
        ),
        out_specs=(
            P(("expert", "dp"), None),
            P(("expert", "dp"), None),
            P("dp", "expert"),
            P("expert", "dp"),
        ),
        check_vma=False,
    )
```

```python
import functools

import jax
import jax.numpy as jnp
from jax import lax
from jax.experimental import pallas as pl
from jax.experimental.pallas import tpu as pltpu
from jax.sharding import PartitionSpec as P

MESH = pl.DeviceIdType.MESH
F32 = jnp.float32
BF16 = jnp.bfloat16

D = 1280
HALF = D // 2
E = 8
Z = 8
DP = 4
GROUPS = 4
LEN = 128
TOK = GROUPS * LEN
BLOCK = 384
COLS = 640
ROWS = E * GROUPS
PAIR = 2 * ROWS
QUARTER = D // DP
RBLOCK = D // E
RSHARE = RBLOCK // (Z * DP)
FAR_A = (5, 3, 4, 2, 6, 1, 7, 0)
FAR_Z = (4, 3, 5, 2, 6, 1, 7)
FAR_DP = (3, 2, 1, 0)


def nn(a, b):
    return lax.dot_general(a, b, (((1,), (0,)), ((), ())), preferred_element_type=F32)


def nt(a, b):
    return lax.dot_general(a, b, (((1,), (1,)), ((), ())), preferred_element_type=F32)


def tn(a, b):
    return lax.dot_general(a, b, (((0,), (0,)), ((), ())), preferred_element_type=F32)


def iota(shape, dim):
    return lax.broadcasted_iota(jnp.int32, shape, dim)


def one_hot(rows, cols, source):
    row = iota((rows, cols), 0)
    return (iota((rows, cols), 1) == source(row)).astype(F32).astype(BF16)


def bits(value, low, count):
    return lax.bitwise_and(lax.shift_right_logical(value, jnp.full_like(value, low)), jnp.full_like(value, count - 1))


def kernel(
    tok_hbm, dout_hbm, saved_hbm, router_hbm, w1_hbm, w2_hbm,
    dtok, drouter_ref, dw1_ref, dw2_ref,
    tok, dout, saved, router, w1, w2,
    a_out, a_in, x, hid, pg, back, rs_out, rs_in, ret_out, ret_in,
    dw, c_out, c_in, y_out, y_in, y_x, y_hid, score_combine,
    r1_out, r1_in, r2_out, r2_in,
    load_sem,
    a_ss, a_rs, g_ss, g_rs, rs_ss, rs_rs, ret_ss, ret_rs,
    c_ss, c_rs, y_ss, y_rs, n_ss, n_rs, r1_ss, r1_rs, r2_ss, r2_rs,
):
    expert = lax.axis_index("expert")
    dp = lax.axis_index("dp")
    a = expert // Z
    z = expert % Z
    y_lo = dp // 2
    core = dp % 2

    def at_a(j):
        return lax.rem(a + j, E)

    def at_z(j):
        return lax.rem(z + j, Z)

    def dev_a(j):
        return (at_a(j) * Z + z, dp)

    def dev_z(j):
        return (a * Z + at_z(j), dp)

    shifts = [(i, j) for i in FAR_A for j in FAR_DP if i or j]
    plane = [(at_a(i) * Z + z, lax.rem(dp + j, DP)) for i, j in shifts]
    other_core = (expert, y_lo * 2 + (1 - core))
    other_chip = (expert, (1 - y_lo) * 2 + core)

    def worker(j):
        return (at_a(j) * Z + z, y_lo * 2 + 1)

    def remote(src, dst, ss, rs, device):
        return pltpu.make_async_remote_copy(
            src_ref=src, dst_ref=dst, send_sem=ss, recv_sem=rs, device_id=device, device_id_type=MESH
        )

    def send(*args):
        remote(*args).start()

    def arrived(ref, sem):
        remote(ref, ref, sem, sem, other_core).wait_recv()

    def sent(ref, sem):
        remote(ref, ref, sem, sem, other_core).wait_send()

    loads = [
        pltpu.make_async_copy(src, dst, load_sem.at[i])
        for i, (src, dst) in enumerate(
            ((router_hbm, router), (dout_hbm, dout), (saved_hbm, saved), (w1_hbm, w1), (w2_hbm, w2))
        )
    ]
    groups = [pl.ds(g * LEN, LEN) for g in range(GROUPS)]
    token_loads = [
        pltpu.make_async_copy(tok_hbm.at[here, :], tok.at[here, :], load_sem.at[5 + g]) for g, here in enumerate(groups)
    ]
    loads[0].start()
    for load in token_loads:
        load.start()
    barrier = pltpu.get_barrier_semaphore()
    greeted = (
        [dev_a(j) for j in range(1, E)]
        + [(at_a(j) * Z + z, y_lo * 2 + 1 - core) for j in range(E)]
        + [dev_z(j) for j in (1, 3, Z - 3, Z - 1)]
        + [(expert, (1 - y_lo) * 2 + c) for c in range(2)]
    )
    for device in greeted:
        pl.semaphore_signal(barrier, inc=1, device_id=device, device_id_type=MESH)

    loads[0].wait()
    loads[1].start()
    loads[2].start()

    @pl.when(core == 1)
    def _():
        loads[3].start()
        loads[4].start()

    logits, parts = [], []
    for load, here in zip(token_loads, groups):
        load.wait()
        logits.append(nt(router[...], tok[here, :]))
    for part in logits:
        part = jnp.exp(part - jnp.max(part, axis=1, keepdims=True))
        parts.append(part / jnp.sum(part, axis=1, keepdims=True))
    logits = jnp.concatenate(logits, axis=1)
    dispatch = jnp.concatenate(parts, axis=1)
    dispatch_b = dispatch.astype(BF16)
    spread = one_hot(ROWS, E, lambda r: bits(r, 2, E))
    own_group = bits(iota((ROWS, TOK), 0), 0, GROUPS) == bits(iota((ROWS, TOK), 1), 7, GROUPS)
    spread_blocks = [
        jnp.where(bits(iota((E * 16, ROWS), 0), 2, 4) == c, one_hot(E * 16, ROWS, lambda r: bits(r, 4, E) * 4 + bits(r, 0, 4)), 0.0).astype(BF16)
        for c in range(4)
    ]

    def messages(slots):
        slots = jnp.concatenate([slots, jnp.zeros((ROWS, 4 * BLOCK - D), BF16)], axis=1)
        total = nn(spread_blocks[0], slots[:, :BLOCK])
        for c in range(1, 4):
            total = total + nn(spread_blocks[c], slots[:, c * BLOCK : (c + 1) * BLOCK])
        return total.astype(BF16).reshape(E, 16, BLOCK)

    def slot_rows(weights, rows):
        pick = jnp.where(own_group, nn(spread, weights), 0.0).astype(BF16)
        return messages(nn(pick, rows).astype(BF16))

    def dispatch_rows(k):
        for j in FAR_A[:-1]:
            send(a_out.at[k, at_a(j)], a_in.at[k, core, a], a_ss.at[k, j], a_rs.at[k, core, j], worker(j))

        @pl.when(core == 0)
        def _():
            send(a_out.at[k, a], a_in.at[k, 0, a], a_ss.at[k, 0], a_rs.at[k, 0, 0], worker(0))

        @pl.when(core == 1)
        def _():
            a_in[k, 1, a] = a_out[k, a]

    a_out[0] = slot_rows(dispatch_b, tok[...])
    pl.semaphore_wait(barrier, len(greeted))
    dispatch_rows(0)
    combine = jnp.exp(logits - jnp.max(logits, axis=0, keepdims=True))
    combine = combine / jnp.sum(combine, axis=0, keepdims=True)
    loads[1].wait()
    a_out[1] = slot_rows(combine.astype(BF16), dout[...])
    dispatch_rows(1)

    def early_score():
        loads[2].wait()
        combine_grad = jnp.concatenate(
            [nt(saved[g], dout[g * LEN : (g + 1) * LEN, :]) for g in range(GROUPS)], axis=1
        )
        score_combine[...] = combine * (combine_grad - jnp.sum(combine * combine_grad, axis=0, keepdims=True))

    def hop(way, r, k, h):
        step = 1 if way == 0 else Z - 1
        held = at_z((Z - step) * (r - 1) % Z)
        send(x.at[k, h, held], x.at[k, h, held], g_ss.at[way, r - 1, k, h], g_rs.at[way, r - 1, k, h], dev_z(step))

    def hop_arrived(way, r, k, h):
        arrived(x.at[k, h, 0], g_rs.at[way, r - 1, k, h])

    def expert_rows(offsets):
        chunks = [at_z(d) for d in offsets]
        for d, c in zip(offsets, chunks):
            send(x.at[1, 1 - y_lo, c], y_x.at[c], n_ss.at[0, d], n_rs.at[0, d], other_chip)
        x_in, x_grad = (
            jnp.concatenate([jnp.concatenate([x[k, h, c] for c in chunks], axis=0) for h in range(2)], axis=1)
            for k in range(2)
        )
        pre = nn(x_in, w1[...])
        hidden_grad = nt(x_grad, w2[...])
        cdf = 0.5 * (1.0 + lax.erf(pre * 0.7071067811865476))
        slope = cdf + pre * jnp.exp(-0.5 * pre * pre) * 0.3989422804014327
        hidden = (pre * cdf).astype(BF16)
        pre_grad = (hidden_grad * slope).astype(BF16)
        grads = nt(pre_grad, w1[...])
        for i, c in enumerate(chunks):
            rows = slice(i * PAIR, (i + 1) * PAIR)
            hid[c] = hidden[rows]
            pg[c] = pre_grad[rows]
            back[c] = grads[rows]
        for d, c in zip(offsets, chunks):
            send(hid.at[c], y_hid.at[c], n_ss.at[1, d], n_rs.at[1, d], other_chip)

    def half(h):
        return slice(h * HALF, (h + 1) * HALF)

    def partial(way, d, h):
        step = 1 if way == 0 else Z - 1
        value = back[at_z(step * d % Z), :, half(h)]
        if d < 3:
            arrived(rs_in.at[way, d, h], rs_rs.at[way, d, h])
            value = value + rs_in[way, d, h].astype(F32)
        if d == 1 and h == way:
            arrived(rs_in.at[way, 3, h], rs_rs.at[way, 3, h])
            value = value + rs_in[way, 3, h].astype(F32)
        rs_out[way, d - 1, h] = value.astype(BF16)
        send(
            rs_out.at[way, d - 1, h], rs_in.at[way, d - 1, h], rs_ss.at[way, d - 1, h], rs_rs.at[way, d - 1, h],
            dev_z(3 * step % Z if d == 4 else step),
        )

    def partials(d, far):
        for way in range(2):
            partial(way, d, way if far else 1 - way)

    def rows_dot(rows, grads):
        return tn(rows.reshape(Z * PAIR, HALF), grads.reshape(Z * PAIR, COLS))

    def share(k, grad):
        dw[k] = grad[QUARTER:]
        c_out[k] = grad[:QUARTER].astype(BF16)
        send(c_out.at[k], c_in.at[k], c_ss.at[k], c_rs.at[k], other_core)

    def other_in():
        y_out[...] = rows_dot(x[0, 1 - y_lo], pg[...]).astype(BF16).reshape(2, QUARTER, COLS)
        for c in range(2):
            send(y_out.at[c], y_in, y_ss.at[c], y_rs, (expert, (1 - y_lo) * 2 + c))

    def own_in():
        share(0, rows_dot(x[0, y_lo], pg[...]))

    def own_out():
        for d in range(Z):
            arrived(y_x.at[0], n_rs.at[0, d])
            arrived(y_hid.at[0], n_rs.at[1, d])
        share(1, rows_dot(x[1, y_lo], hid[...]) + rows_dot(y_x[...], y_hid[...]))

    @pl.when(core == 0)
    def _():
        early_score()

    @pl.when(core == 1)
    def _():
        order = one_hot(
            4 * PAIR, 4 * PAIR,
            lambda r: bits(r, 5, 2) * 128 + bits(r, 2, 8) * 16 + bits(r, 6, 4) * 4 + bits(r, 0, 4),
        )
        for k in range(2):
            for c in range(2):
                for j in range(c, E):
                    arrived(a_in.at[k, c, 0], a_rs.at[k, c, j])
            chunk = nn(order, a_in[k].reshape(4 * PAIR, BLOCK)).astype(BF16)
            chunk = jnp.concatenate([chunk[b * PAIR : (b + 1) * PAIR] for b in range(4)], axis=1)
            for h in range(2):
                x[k, h, z] = chunk[:, half(h)]
                for way in range(2):
                    hop(way, 1, k, h)
        early_score()
        loads[3].wait()
        loads[4].wait()
        for r in range(1, 4):
            for k in range(2):
                for h in range(2):
                    for way in range(2):
                        hop_arrived(way, r, k, h)
                        if r < 3 or way == k:
                            hop(way, r + 1, k, h)
            expert_rows(([0] if r == 1 else []) + [Z - r, r])
        partials(3, False)
        partials(3, True)
        for k in range(2):
            for h in range(2):
                hop_arrived(k, 4, k, h)
        expert_rows([4])

        partials(4, True)
        other_in()
        partials(2, False)
        partials(2, True)
        partials(1, False)
        partials(1, True)

        halves = []
        for h in range(2):
            value = back[z, :, half(h)]
            for way in range(2):
                arrived(rs_in.at[way, 0, h], rs_rs.at[way, 0, h])
                value = value + rs_in[way, 0, h].astype(F32)
            halves.append(value.astype(BF16))
        total = jnp.concatenate(halves, axis=1)
        for c in range(2):
            ret_out[c] = messages(total[c * ROWS : (c + 1) * ROWS])
            for j in FAR_A[: E - c]:
                send(
                    ret_out.at[c, at_a(j)], ret_in.at[a], ret_ss.at[c, j], ret_rs.at[j],
                    (at_a(j) * Z + z, y_lo * 2 + c),
                )
        ret_in[a] = ret_out[1, a]
        own_in()
        own_out()

    order = one_hot(4 * ROWS, 4 * ROWS, lambda r: bits(r, 0, 8) * 16 + bits(r, 5, 4) * 4 + bits(r, 3, 4))
    for j in range(1, E):
        arrived(ret_in.at[0], ret_rs.at[j])

    @pl.when(core == 0)
    def _():
        arrived(ret_in.at[0], ret_rs.at[0])

    mixed = nn(order, ret_in[...].reshape(4 * ROWS, BLOCK))
    slot_grads = jnp.concatenate([mixed[c * ROWS : (c + 1) * ROWS] for c in range(4)], axis=1)[:, :D]

    parts = []
    for g in range(GROUPS):
        here = slice(g * LEN, (g + 1) * LEN)
        grad = nt(slot_grads[g * E : (g + 1) * E].astype(BF16), tok[here, :])
        weight = dispatch[:, here]
        parts.append(weight * (grad - jnp.sum(weight * grad, axis=1, keepdims=True)))
    score = (score_combine[...] + jnp.concatenate(parts, axis=1)).astype(BF16)

    router_grad = nn(score, tok[...])
    for b in range(E):
        columns = router_grad[:, b * RBLOCK : (b + 1) * RBLOCK]
        columns = jnp.concatenate([columns, jnp.zeros((E, 256 - RBLOCK), F32)], axis=1)
        r1_out[b] = jnp.concatenate([columns[:, :128], columns[:, 128:]], axis=0).astype(BF16)
    for i, device in enumerate(plane):
        send(r1_out.at[at_a(shifts[i][0])], r1_in.at[a * DP + dp], r1_ss.at[i], r1_rs.at[i], device)

    router_f = router[...].astype(F32)
    for g in range(GROUPS):
        here = slice(g * LEN, (g + 1) * LEN)
        left = jnp.concatenate([dispatch_b[:, here].astype(F32), score[:, here].astype(F32)], axis=0).astype(BF16)
        right = jnp.concatenate([slot_grads[g * E : (g + 1) * E], router_f], axis=0).astype(BF16)
        dtok[here, :] = tn(left, right).astype(BF16)

    for k in range(2):
        for j in range(1, E):
            sent(a_out.at[k, 0], a_ss.at[k, j])

    @pl.when(core == 0)
    def _():
        for k in range(2):
            sent(a_out.at[k, 0], a_ss.at[k, 0])

    @pl.when(core == 1)
    def _():
        for way in range(2):
            for k in range(2):
                for h in range(2):
                    for r in range(1, 5 if way == k else 4):
                        sent(x.at[k, h, 0], g_ss.at[way, r - 1, k, h])
            for h in range(2):
                for d in range(1, 5 if way == h else 4):
                    sent(rs_out.at[way, d - 1, h], rs_ss.at[way, d - 1, h])
        for k in range(2):
            sent(c_out.at[k], c_ss.at[k])
            sent(y_out.at[k], y_ss.at[k])
            for d in range(Z):
                sent(hid.at[0], n_ss.at[k, d])
        for c in range(2):
            for j in range(c, E):
                sent(ret_out.at[c, 0], ret_ss.at[c, j])

    total = r1_out[a].astype(F32)
    for n, (i, j) in enumerate(shifts):
        arrived(r1_in.at[0], r1_rs.at[n])
        total = total + r1_in[at_a(E - i) * DP + lax.rem(dp + DP - j, DP)].astype(F32)
    r2_out[...] = total.astype(BF16)
    for j in FAR_Z:
        send(r2_out, r2_in.at[z], r2_ss.at[j - 1], r2_rs.at[j - 1], dev_z(j))

    for n in range(E * DP - 1):
        sent(r1_out.at[0], r1_ss.at[n])
    arrived(y_in, y_rs)

    @pl.when(core == 0)
    def _():
        for k in range(2):
            arrived(c_in.at[k], c_rs.at[k])
        dw1_ref[...] = c_in[0].astype(F32) + y_in[...].astype(F32)
        dw2_ref[...] = c_in[1].astype(F32)

    @pl.when(core == 1)
    def _():
        dw1_ref[...] = dw[0] + y_in[...].astype(F32)
        dw2_ref[...] = dw[1]

    for j in range(1, Z):
        arrived(r2_in.at[0], r2_rs.at[j - 1])
        total = total + r2_in[at_z(Z - j)].astype(F32)
    total = jnp.concatenate([total[:E], total[E:]], axis=1)
    first = (z * DP + dp) * RSHARE
    pick = (iota((E, 256), 1) == first + iota((E, 256), 0)).astype(F32)
    mine = lax.dot_general(
        pick, total, (((1,), (1,)), ((), ())), precision=lax.Precision.HIGHEST, preferred_element_type=F32
    )
    drouter_ref[...] = mine[:RSHARE]

    for n in range(Z - 1):
        sent(r2_out, r2_ss.at[n])


def deliver(*refs):
    sources, targets, sems = refs[:4], refs[4:8], refs[8]
    copies = [pltpu.make_async_copy(s, t, sems.at[i]) for i, (s, t) in enumerate(zip(sources, targets))]
    for copy in copies:
        copy.start()
    for copy in copies:
        copy.wait()


def shards(tokens, d_out, slot_outputs, router, w_in, w_out):
    dma = pltpu.SemaphoreType.DMA
    vmem = pltpu.VMEM
    outs = (
        jax.ShapeDtypeStruct((TOK, D), BF16),
        jax.ShapeDtypeStruct((RSHARE, E), F32),
        jax.ShapeDtypeStruct((QUARTER, COLS), F32),
        jax.ShapeDtypeStruct((QUARTER, COLS), F32),
    )
    results = pl.pallas_call(
        kernel,
        out_shape=tuple(vmem(o.shape, o.dtype) for o in outs),
        in_specs=[pl.BlockSpec(memory_space=pltpu.HBM)] * 6,
        out_specs=(pl.BlockSpec(memory_space=pltpu.VMEM),) * 4,
        scratch_shapes=[
            vmem((TOK, D), BF16),
            vmem((TOK, D), BF16),
            vmem((GROUPS, E, D), BF16),
            vmem((E, D), BF16),
            vmem((D, COLS), BF16),
            vmem((COLS, D), BF16),
            vmem((2, E, 16, BLOCK), BF16),
            vmem((2, 2, E, 16, BLOCK), BF16),
            vmem((2, 2, Z, PAIR, HALF), BF16),
            vmem((Z, PAIR, COLS), BF16),
            vmem((Z, PAIR, COLS), BF16),
            vmem((Z, PAIR, D), F32),
            vmem((2, 4, 2, PAIR, HALF), BF16),
            vmem((2, 4, 2, PAIR, HALF), BF16),
            vmem((2, E, 16, BLOCK), BF16),
            vmem((E, 16, BLOCK), BF16),
            vmem((2, QUARTER, COLS), F32),
            vmem((2, QUARTER, COLS), BF16),
            vmem((2, QUARTER, COLS), BF16),
            vmem((2, QUARTER, COLS), BF16),
            vmem((QUARTER, COLS), BF16),
            vmem((Z, PAIR, HALF), BF16),
            vmem((Z, PAIR, COLS), BF16),
            vmem((E, TOK), F32),
            vmem((E, 16, 128), BF16),
            vmem((E * DP, 16, 128), BF16),
            vmem((16, 128), BF16),
            vmem((Z, 16, 128), BF16),
            dma((5 + GROUPS,)),
            dma((2, E)),
            dma((2, 2, E)),
            dma((2, 4, 2, 2)),
            dma((2, 4, 2, 2)),
            dma((2, 4, 2)),
            dma((2, 4, 2)),
            dma((2, E)),
            dma((E,)),
            dma((2,)),
            dma((2,)),
            dma((2,)),
            dma,
            dma((2, Z)),
            dma((2, Z)),
            dma((E * DP - 1,)),
            dma((E * DP - 1,)),
            dma((Z - 1,)),
            dma((Z - 1,)),
        ],
        compiler_params=pltpu.CompilerParams(
            collective_id=0, has_side_effects=True, vmem_limit_bytes=63_900_000
        ),
    )(tokens, d_out, slot_outputs, router.T, w_in, w_out)
    d_tokens, d_router, d_w_in, d_w_out_t = pl.pallas_call(
        deliver,
        out_shape=outs,
        in_specs=[pl.BlockSpec(memory_space=pl.ANY)] * 4,
        out_specs=(pl.BlockSpec(memory_space=pl.ANY),) * 4,
        scratch_shapes=[dma((4,))],
        compiler_params=pltpu.CompilerParams(vmem_limit_bytes=1024 * 1024),
    )(*results)
    return (d_tokens, d_router, d_w_in, d_w_out_t.T)


def solution(mesh):
    return jax.shard_map(
        shards,
        mesh=mesh,
        in_specs=(
            P(("expert", "dp"), None),
            P(("expert", "dp"), None),
            P(("expert", "dp"), None, None),
            P(),
            P(None, "expert"),
            P("expert", None),
        ),
        out_specs=(
            P(("expert", "dp"), None),
            P(("expert", "dp"), None),
            P("dp", "expert"),
            P("expert", "dp"),
        ),
        check_vma=False,
    )
```
